32 devices in a mesh: tile: 16 (over z, y, x), narrow: 2 (over core).
Axes of the slice: x: 2, y: 2, z: 4, core: 2. Of those that a mesh axis runs over, the one named last changes fastest.
Arguments:
- fine: bfloat16 [256, 16, 512], P('tile', 'narrow'), may hold values from -6 to 6
- coarse: bfloat16 [64, 128, 1024], P('tile'), may hold values from -6 to 6
- block_table: int32 [16, 8], P('tile'), may hold values from 0 to 63, as said below
- shifts: int32 [2], replicated, may hold values from 1 to 7
- attn_gain: float32 [512], replicated, may hold values from 0.1 to 1.9
- w_query: bfloat16 [512, 512], replicated, may hold values from -8 to 8
- w_key: bfloat16 [512, 512], replicated, may hold values from -8 to 8
- w_value: bfloat16 [512, 512], replicated, may hold values from -0.25 to 0.25
- w_out: bfloat16 [512, 512], replicated, may hold values from -0.25 to 0.25
- coarse_key: bfloat16 [1024, 512], replicated, may hold values from -0.1875 to 0.1875
- coarse_value: bfloat16 [1024, 512], replicated, may hold values from -0.1875 to 0.1875
- mlp_gain: float32 [512], replicated, may hold values from 0.1 to 1.9
- w_gate: bfloat16 [512, 2048], replicated, may hold values from -0.25 to 0.25
- w_up: bfloat16 [512, 2048], replicated, may hold values from -0.25 to 0.25
- w_down: bfloat16 [2048, 512], replicated, may hold values from -0.125 to 0.125
Outputs:
- output: bfloat16 [256, 16, 512], P('tile', 'narrow')
The draws below stay inside these ranges and needn't reach their ends.
Inputs may be any that keep to these rules, and one draw needn't show every extreme that they name: `block_table`: row s names 8 distinct blocks, all among blocks (s - 1) * 4 to (s + 2) * 4 - 1 taken modulo 64, at least one of them below s * 4 and at least one at or above (s + 1) * 4 in that range.
All inputs are finite; a program needn't handle non-finite values.
Results may differ from the reference program's by a relative error of at most 0.0073.
Values may be sent and summed in bfloat16 or wider, within the bound.
A program may use at most 64 MiB of HBM per device.

```python
import jax
import jax.numpy as jnp
from jax import lax

FD = 512
HEADS = 8
CW = 1024
FF = 2048
WS = 8
SR = 16
CT = 128
CB_DEV = 4
NB = 8
HD = 64
SC = 16
STRIPS = 16
ROWS = 256
CBLOCKS = 64


def draw_block_table(key, part):
    key = jax.random.fold_in(key, 11)
    span = 3 * CB_DEV
    position = jnp.arange(span, dtype=jnp.int32)[None, :]
    scores = jax.random.randint(jax.random.fold_in(key, 1), (STRIPS, span), 0, 1 << 20) * span + position
    lower_pick = jax.random.randint(jax.random.fold_in(key, 2), (STRIPS, 1), 0, CB_DEV)
    upper_pick = jax.random.randint(jax.random.fold_in(key, 3), (STRIPS, 1), 0, CB_DEV) + 2 * CB_DEV
    forced = (position == lower_pick) | (position == upper_pick)
    scores = jnp.where(forced, position - 2 * span, scores)
    order = jnp.argsort(scores, axis=1)[:, :NB].astype(jnp.int32)
    first = (jnp.arange(STRIPS, dtype=jnp.int32) - 1) * CB_DEV
    return jnp.mod(first[:, None] + order, CBLOCKS).astype(jnp.int32)


def draw_fine(key, part):
    key = jax.random.fold_in(key, 21)
    noise = jax.random.normal(jax.random.fold_in(key, 1), (ROWS, SC, FD), jnp.float32)
    return jnp.clip(noise, -6.0, 6.0).astype(jnp.bfloat16)


def draw_w_query(key, part):
    key = jax.random.fold_in(key, 31)
    matrix = jax.random.normal(key, (FD, FD), jnp.float32) * FD ** (-0.5)
    return jnp.clip(matrix, -8.0, 8.0).astype(jnp.bfloat16)


def draw_w_key(key, part):
    key = jax.random.fold_in(key, 41)
    matrix = jax.random.normal(key, (FD, FD), jnp.float32) * FD ** (-0.5)
    return jnp.clip(matrix, -8.0, 8.0).astype(jnp.bfloat16)


def block_levels(rng, extent, pieces, low, high):
    def one(dim, parts):
        draws = jax.random.uniform(jax.random.fold_in(jax.random.fold_in(rng, 6), dim), (parts,), jnp.float32, low / len(pieces), high / len(pieces))
        return jnp.repeat(jnp.exp(draws), extent[dim] // parts).reshape((-1,) + (1,) * (len(extent) - dim - 1))

    loudness = one(*pieces[0])
    for cut in pieces[1:]:
        loudness = loudness * one(*cut)
    return loudness


def gaussian(own_key, dims, scale, most, split=(), held_as=jnp.bfloat16):
    drawn = jax.random.normal(own_key, dims, jnp.float32) * scale
    if len(split) > 0:
        drawn = block_levels(own_key, dims, split, -0.22, 0.18) * drawn
    return jnp.clip(drawn, min=-most, max=most).astype(held_as)


def setup_inputs(seed: int = 0) -> dict:
    streams_of = jax.random.split(jax.random.key(seed), 16)
    fine = draw_fine(jax.random.fold_in(streams_of[15], 71), 0)
    coarse = gaussian(streams_of[1], (CBLOCKS, CT, CW), 1.0, 6.0, ((0, 16),))
    block_table = draw_block_table(jax.random.fold_in(streams_of[15], 71), 0)
    shifts = jax.random.randint(streams_of[3], (2,), 1, WS).astype(jnp.int32)
    attn_gain = jnp.clip(1.0 + 0.18 * jax.random.normal(streams_of[4], (FD,), jnp.float32), 0.1, 1.9)
    w_query = draw_w_query(jax.random.fold_in(streams_of[15], 71), 0)
    w_key = draw_w_key(jax.random.fold_in(streams_of[15], 71), 0)
    w_value = gaussian(streams_of[7], (FD, FD), FD ** -0.5, 0.25)
    w_out = gaussian(streams_of[8], (FD, FD), FD ** -0.5, 0.25)
    coarse_key = gaussian(streams_of[9], (CW, FD), CW ** -0.5, 0.1875)
    coarse_value = gaussian(streams_of[10], (CW, FD), CW ** -0.5, 0.1875)
    mlp_gain = jnp.clip(1.0 + 0.18 * jax.random.normal(streams_of[11], (FD,), jnp.float32), 0.1, 1.9)
    w_gate = gaussian(streams_of[12], (FD, FF), FD ** -0.5, 0.25)
    w_up = gaussian(streams_of[13], (FD, FF), FD ** -0.5, 0.25)
    w_down = gaussian(streams_of[14], (FF, FD), FF ** -0.5, 0.125)
    return {"fine": fine, "coarse": coarse, "block_table": block_table, "shifts": shifts, "attn_gain": attn_gain, "w_query": w_query, "w_key": w_key, "w_value": w_value, "w_out": w_out, "coarse_key": coarse_key, "coarse_value": coarse_value, "mlp_gain": mlp_gain, "w_gate": w_gate, "w_up": w_up, "w_down": w_down}


def rms_scale(source, gain_vec):
    values = source.astype(jnp.float32)
    mean_square = lax.optimization_barrier(jnp.mean(values * values, axis=-1, keepdims=True))
    return values * lax.rsqrt(mean_square + 1e-06) * gain_vec.astype(jnp.float32)

def to_windows(source):
    lead_count = source.shape[0] // WS
    across = source.shape[1] // WS
    reordered = source.reshape((lead_count, WS, across, WS) + source.shape[2:])
    reordered = jnp.swapaxes(reordered, 1, 2)
    return reordered.reshape((lead_count * across, WS * WS) + source.shape[2:])

def from_windows(source, row_count, column_count):
    reordered = source.reshape((row_count // WS, column_count // WS, WS, WS) + source.shape[2:])
    reordered = jnp.swapaxes(reordered, 1, 2)
    return reordered.reshape((row_count, column_count) + source.shape[2:])

def attend(queries, keys_fine, values_fine, coarse_keys, coarse_values, row_flag, column_flag):
    row_count, column_count = (queries.shape[0], queries.shape[1])
    labels = row_flag.astype(jnp.int32)[:, None] * 2 + column_flag.astype(jnp.int32)[None, :]
    labels = to_windows(labels)
    allowed = labels[:, :, None] == labels[:, None, :]
    query_win = to_windows(queries).astype(jnp.float32)
    key_win = to_windows(keys_fine).astype(jnp.float32)
    value_win = to_windows(values_fine).astype(jnp.float32)
    score_self = jnp.einsum('wqhd,wkhd->whqk', query_win, key_win)
    score_self = jnp.where(allowed[:, None], score_self, -jnp.inf)
    score_cross = jnp.einsum('wqhd,khd->whqk', query_win, coarse_keys.astype(jnp.float32))
    maxima = jnp.maximum(lax.optimization_barrier(jnp.max(score_self, axis=-1, keepdims=True)), lax.optimization_barrier(jnp.max(score_cross, axis=-1, keepdims=True)))
    exp_self = jnp.exp(score_self - maxima)
    exp_cross = jnp.exp(score_cross - maxima)
    totals = lax.optimization_barrier(jnp.sum(exp_self, axis=-1, keepdims=True)) + lax.optimization_barrier(jnp.sum(exp_cross, axis=-1, keepdims=True))
    prob_self = (exp_self / totals).astype(jnp.bfloat16).astype(jnp.float32)
    prob_cross = (exp_cross / totals).astype(jnp.bfloat16).astype(jnp.float32)
    mixture = jnp.einsum('whqk,wkhd->wqhd', prob_self, value_win)
    mixture = mixture + jnp.einsum('whqk,khd->wqhd', prob_cross, coarse_values.astype(jnp.float32))
    return from_windows(mixture.astype(jnp.bfloat16), row_count, column_count)

def reference(fine, coarse, block_table, shifts, attn_gain, w_query, w_key, w_value, w_out, coarse_key, coarse_value, mlp_gain, w_gate, w_up, w_down):
    shift_row = shifts[0]
    shift_col = shifts[1]
    row_total, column_count = (fine.shape[0], fine.shape[1])
    rolled = jnp.roll(fine, (-shift_row, -shift_col), axis=(0, 1))
    flat_rows = rolled.reshape(-1, FD)
    normed = rms_scale(flat_rows, attn_gain).astype(jnp.bfloat16)
    query_scale = 1.0 / HD ** 0.5
    queries = (jnp.dot(normed, w_query, preferred_element_type=jnp.float32) * query_scale).astype(jnp.bfloat16)
    keys_fine = jnp.dot(normed, w_key, preferred_element_type=jnp.float32).astype(jnp.bfloat16)
    values_fine = jnp.dot(normed, w_value, preferred_element_type=jnp.float32).astype(jnp.bfloat16)
    queries = queries.reshape(row_total, column_count, HEADS, HD)
    keys_fine = keys_fine.reshape(row_total, column_count, HEADS, HD)
    values_fine = values_fine.reshape(row_total, column_count, HEADS, HD)
    coarse_flat = coarse.reshape(-1, CW)
    coarse_keys = jnp.dot(coarse_flat, coarse_key, preferred_element_type=jnp.float32).astype(jnp.bfloat16).reshape(CBLOCKS, CT, HEADS, HD)
    coarse_values = jnp.dot(coarse_flat, coarse_value, preferred_element_type=jnp.float32).astype(jnp.bfloat16).reshape(CBLOCKS, CT, HEADS, HD)
    row_flags = jnp.arange(row_total, dtype=jnp.int32) + shift_row >= row_total
    column_flag = jnp.arange(column_count, dtype=jnp.int32) + shift_col >= column_count

    def one_strip(strip_index):
        start_row = (strip_index * SR).astype(jnp.int32)
        picked = block_table[strip_index]
        strip_keys = coarse_keys[picked].reshape(NB * CT, HEADS, HD)
        strip_values = coarse_values[picked].reshape(NB * CT, HEADS, HD)
        return attend(lax.dynamic_slice_in_dim(queries, start_row, SR, 0), lax.dynamic_slice_in_dim(keys_fine, start_row, SR, 0), lax.dynamic_slice_in_dim(values_fine, start_row, SR, 0), strip_keys, strip_values, lax.dynamic_slice_in_dim(row_flags, start_row, SR, 0), column_flag)
    head_out = lax.map(one_strip, jnp.arange(STRIPS, dtype=jnp.int32)).reshape(-1, FD)
    attn_sum = jnp.dot(head_out, w_out, preferred_element_type=jnp.float32)
    mid = flat_rows.astype(jnp.float32) + attn_sum
    normed_mid = rms_scale(mid, mlp_gain).astype(jnp.bfloat16)
    gate_term = jnp.dot(normed_mid, w_gate, preferred_element_type=jnp.float32)
    up_term = jnp.dot(normed_mid, w_up, preferred_element_type=jnp.float32)
    hidden = (jax.nn.silu(gate_term) * up_term).astype(jnp.bfloat16)
    mlp_sum = jnp.dot(hidden, w_down, preferred_element_type=jnp.float32)
    block_out = (mid + mlp_sum).astype(jnp.bfloat16).reshape(row_total, column_count, FD)
    return jnp.roll(block_out, (shift_row, shift_col), axis=(0, 1))
```

```python
import functools

import jax
import jax.numpy as jnp
from jax import lax
from jax.experimental import pallas as pl
from jax.experimental.pallas import tpu as pltpu
from jax.sharding import PartitionSpec as P

WS = 8
HD = 64
HEADS = 8
PAIR = 2 * HD
CT = 128
NB = 8
HIDDEN = -1e30
MESH = pl.DeviceIdType.MESH
F32 = jnp.float32
BF16 = jnp.bfloat16


def dot(a, b):
    return jnp.dot(a, b, preferred_element_type=F32)


def rms_scale(values, gain_vec):
    mean_square = jnp.mean(values * values, axis=-1, keepdims=True)
    return values * lax.rsqrt(mean_square + 1e-06) * gain_vec


def one_hot_rows(index, count):
    lanes = lax.broadcasted_iota(jnp.int32, (index.shape[0], count), 1)
    return (lanes == index).astype(F32).astype(BF16)


def paired(q_t):
    zero = jnp.zeros((HD, q_t.shape[1]), q_t.dtype)
    upper = jnp.concatenate([q_t[:HD], zero], axis=1)
    lower = jnp.concatenate([zero, q_t[HD:]], axis=1)
    return jnp.concatenate([upper, lower], axis=0)


def unpaired(both, tokens):
    return jnp.concatenate([both[:HD, :tokens], both[HD:, tokens:]], axis=0)


def kernel(
    tiles,
    narrows,
    table,
    shifts,
    fine,
    coarse,
    attn_gain,
    w_query,
    w_key,
    w_value,
    w_out,
    coarse_key,
    coarse_value,
    mlp_gain,
    w_gate,
    w_up,
    w_down,
    out,
    ext,
    back,
    coarse_v,
    gain1_v,
    wq_v,
    wk_v,
    wv_v,
    wo_v,
    ck_v,
    cv_v,
    gain2_v,
    wg_v,
    wu_v,
    wd_v,
    keys_v,
    values_t,
    q_send,
    q_from_prev,
    q_from_next,
    o_send,
    st_send,
    o_recv,
    st_recv,
    own_o,
    own_st,
    load_sem,
    send_sem,
    recv_sem,
):
    s = lax.axis_index("tile")
    n = lax.axis_index("narrow")
    s_next, s_prev = lax.rem(s + 1, tiles), lax.rem(s + tiles - 1, tiles)
    n_next, n_prev = lax.rem(n + 1, narrows), lax.rem(n + narrows - 1, narrows)
    tokens, width = fine.shape
    half = WS * WS
    rows_dev = tokens // WS
    blocks = coarse.shape[0] // CT

    barrier = pltpu.get_barrier_semaphore()
    for peer in (
        (s, n_next),
        (s, n_prev),
        (s_next, n),
        (s_prev, n),
        (s_next, n_next),
        (s_prev, n_prev),
    ):
        pl.semaphore_signal(barrier, inc=1, device_id=peer, device_id_type=MESH)

    pairs = (
        (coarse, coarse_v),
        (coarse_key, ck_v),
        (coarse_value, cv_v),
        (fine, ext.at[pl.ds(0, tokens)]),
        (attn_gain, gain1_v),
        (w_query, wq_v),
        (w_key, wk_v),
        (w_value, wv_v),
        (w_out, wo_v),
        (mlp_gain, gain2_v),
        (w_gate, wg_v),
        (w_up, wu_v),
        (w_down, wd_v),
    )
    loads = [
        pltpu.make_async_copy(src, dst, load_sem.at[i]) for i, (src, dst) in enumerate(pairs)
    ]
    for load in loads:
        load.start()

    def remote(slot, src, dst, peer):
        return pltpu.make_async_remote_copy(
            src_ref=src,
            dst_ref=dst,
            send_sem=send_sem.at[slot],
            recv_sem=recv_sem.at[slot],
            device_id=peer,
            device_id_type=MESH,
        )

    pl.semaphore_wait(barrier, 6)
    first = fine.at[pl.ds(0, half)]
    fine_copies = (
        remote(0, first, ext.at[pl.ds(2 * tokens, half)], (s_prev, n)),
        remote(1, first, ext.at[pl.ds(2 * tokens + half, half)], (s_prev, n_prev)),
        remote(2, fine, ext.at[pl.ds(tokens, tokens)], (s, n_prev)),
    )
    for copy in fine_copies:
        copy.start()

    shift_row = shifts[0]
    shift_col = shifts[1]

    total = blocks * tiles
    entries = [
        lax.rem(table[0, i] - (s - 1) * blocks + total, total) for i in range(NB)
    ]

    def block_bias(j):
        hit = entries[0] == j
        for e in entries[1:]:
            hit = hit | (e == j)
        return jnp.where(hit, 0.0, HIDDEN).astype(F32)

    bias = [block_bias(j) for j in range(3 * blocks)]

    def bias_rows(values):
        row = lax.broadcasted_iota(jnp.int32, (16, tokens), 0)
        filled = jnp.zeros((16, tokens), F32)
        for b, value in enumerate(values):
            filled = jnp.where(row == b, value, filled)
        return filled.astype(BF16)

    q_send[pl.ds(0, 16), :] = bias_rows(bias[2 * blocks :])
    q_send[pl.ds(16 + width, 16), :] = bias_rows(bias[:blocks])

    for i in range(3):
        loads[i].wait()
    keys_v[...] = dot(coarse_v[...], ck_v[...]).astype(BF16)
    values_t[...] = dot(coarse_v[...], cv_v[...]).T.astype(BF16)

    for i in range(3, 8):
        loads[i].wait()
    for copy in fine_copies:
        copy.wait()

    t = lax.broadcasted_iota(jnp.int32, (tokens, 1), 0)
    row = (t >> 3) + shift_row
    col = (t & 7) + shift_col
    right = jnp.where(col >= WS, 1, 0)
    below = jnp.where(row >= rows_dev, 1, 0)
    place = (
        (row - below * rows_dev) * WS
        + (col - right * WS)
        + below * 2 * tokens
        + right * jnp.where(row >= rows_dev, half, tokens)
    )
    rolled = dot(one_hot_rows(place, 3 * tokens), ext[...])
    normed = rms_scale(rolled, gain1_v[...]).astype(BF16)
    queries = dot(normed, wq_v[...]) * (1.0 / HD**0.5)
    q_send[pl.ds(16, width), :] = queries.T.astype(BF16)
    q_copies = (
        remote(3, q_send.at[pl.ds(0, 16 + width)], q_from_prev, (s_next, n)),
        remote(4, q_send.at[pl.ds(16, 16 + width)], q_from_next, (s_prev, n)),
    )
    for copy in q_copies:
        copy.start()

    keys_fine = dot(normed, wk_v[...]).astype(BF16)
    values_fine_t = dot(normed, wv_v[...]).T.astype(BF16)

    def label(axis):
        i = lax.broadcasted_iota(jnp.int32, (tokens, tokens), axis)
        r = s * rows_dev + (i >> 3) + shift_row
        c = n * WS + (i & 7) + shift_col
        window = (i >> 6) * 4
        return (
            window
            + jnp.where(r >= rows_dev * tiles, 2, 0)
            + jnp.where(c >= WS * narrows, 1, 0)
        )

    self_bias = jnp.where(label(0) == label(1), 0.0, HIDDEN).astype(F32)
    self_bias = jnp.concatenate([self_bias, self_bias], axis=1)

    def attend(pair, q_t, biases, with_self):
        at = slice(pair * PAIR, (pair + 1) * PAIR)
        q_pair = paired(q_t)
        scores = dot(keys_v[:, at], q_pair)
        parts = [scores[b * CT : (b + 1) * CT] for b in range(blocks)]
        top = None
        for part, hide in zip(parts, biases):
            high = jnp.max(part, axis=0, keepdims=True) + hide
            top = high if top is None else jnp.maximum(top, high)
        if with_self:
            own = dot(keys_fine[:, at], q_pair) + self_bias
            top = jnp.maximum(top, jnp.max(own, axis=0, keepdims=True))
        parts = [jnp.exp(part - (top - hide)) for part, hide in zip(parts, biases)]
        amount = sum(jnp.sum(part, axis=0, keepdims=True) for part in parts)
        mixed = dot(values_t[at, :], jnp.concatenate(parts, axis=0).astype(BF16))
        if with_self:
            own = jnp.exp(own - top)
            amount = amount + jnp.sum(own, axis=0, keepdims=True)
            mixed = mixed + dot(values_fine_t[at, :], own.astype(BF16))
        return top, amount, unpaired(mixed, tokens)

    def split_heads(rows):
        halves = []
        for row in rows:
            halves += [row[:, :tokens], row[:, tokens:]]
        return jnp.concatenate(halves, axis=0)

    def neighbour(slot, q_ref, q_at, bias_at):
        loaded = q_ref[pl.ds(bias_at, 16), :].astype(F32)
        wide = jnp.concatenate([loaded, loaded], axis=1)
        biases = [wide[b : b + 1, :] for b in range(blocks)]
        tops, amounts = [], []
        for pair in range(HEADS // 2):
            q_t = q_ref[pl.ds(q_at + pair * PAIR, PAIR), :]
            top, amount, mixed = attend(pair, q_t, biases, False)
            o_send[slot, pl.ds(pair * PAIR, PAIR), :] = mixed.astype(BF16)
            tops.append(top)
            amounts.append(amount)
        st_send[slot, pl.ds(0, HEADS), :] = split_heads(tops)
        st_send[slot, pl.ds(HEADS, HEADS), :] = split_heads(amounts)

    q_copies[0].wait_recv()
    neighbour(0, q_from_prev, 16, 0)
    part_copies = [
        remote(5, st_send.at[0], st_recv.at[0], (s_prev, n)),
        remote(6, o_send.at[0], o_recv.at[0], (s_prev, n)),
    ]
    for copy in part_copies:
        copy.start()
    q_copies[1].wait_recv()
    neighbour(1, q_from_next, 0, width)
    more = [
        remote(7, st_send.at[1], st_recv.at[1], (s_next, n)),
        remote(8, o_send.at[1], o_recv.at[1], (s_next, n)),
    ]
    for copy in more:
        copy.start()
    part_copies += more

    tops, amounts = [], []
    for pair in range(HEADS // 2):
        q_t = q_send[pl.ds(16 + pair * PAIR, PAIR), :]
        top, amount, mixed = attend(pair, q_t, bias[blocks : 2 * blocks], True)
        own_o[pl.ds(pair * PAIR, PAIR), :] = mixed
        tops.append(top)
        amounts.append(amount)
    own_top, own_amount = split_heads(tops), split_heads(amounts)

    for i in range(8, len(loads)):
        loads[i].wait()
    for copy in q_copies:
        copy.wait_send()
    for copy in part_copies:
        copy.wait()

    all_tops = [own_top] + [st_recv[i, pl.ds(0, HEADS), :] for i in range(2)]
    all_amounts = [own_amount] + [st_recv[i, pl.ds(HEADS, HEADS), :] for i in range(2)]
    top = jnp.maximum(jnp.maximum(all_tops[0], all_tops[1]), all_tops[2])
    scales = [jnp.exp(x - top) for x in all_tops]
    amount = sum(a * b for a, b in zip(scales, all_amounts))
    scales = [x / amount for x in scales]
    heads = []
    for h in range(HEADS):
        at = pl.ds(h * HD, HD)
        heads.append(
            own_o[at, :] * scales[0][h : h + 1]
            + o_recv[0, at, :].astype(F32) * scales[1][h : h + 1]
            + o_recv[1, at, :].astype(F32) * scales[2][h : h + 1]
        )
    head_out = jnp.concatenate(heads, axis=0).T.astype(BF16)
    mid = rolled + dot(head_out, wo_v[...])
    normed_mid = rms_scale(mid, gain2_v[...]).astype(BF16)
    gate = dot(normed_mid, wg_v[...])
    up = dot(normed_mid, wu_v[...])
    hidden = (gate * lax.logistic(gate) * up).astype(BF16)
    block_out = mid + dot(hidden, wd_v[...])
    back[pl.ds(0, tokens), :] = block_out.astype(BF16)

    last = back.at[pl.ds(tokens - half, half)]
    back_copies = (
        remote(9, last, back.at[pl.ds(2 * tokens, half)], (s_next, n)),
        remote(10, last, back.at[pl.ds(2 * tokens + half, half)], (s_next, n_next)),
        remote(11, back.at[pl.ds(0, tokens)], back.at[pl.ds(tokens, tokens)], (s, n_next)),
    )
    for copy in back_copies:
        copy.start()
    row = (t >> 3) - shift_row
    col = (t & 7) - shift_col
    left = jnp.where(col < 0, 1, 0)
    above = jnp.where(row < 0, 1, 0)
    place = (
        (row + above * WS) * WS
        + (col + left * WS)
        + above * 2 * tokens
        + left * jnp.where(row < 0, half, tokens)
    )
    chosen = one_hot_rows(place, 3 * tokens)
    for copy in back_copies:
        copy.wait()
    out[...] = dot(chosen, back[...]).astype(BF16)


def local(
    tiles,
    narrows,
    fine,
    coarse,
    block_table,
    shifts,
    attn_gain,
    w_query,
    w_key,
    w_value,
    w_out,
    coarse_key,
    coarse_value,
    mlp_gain,
    w_gate,
    w_up,
    w_down,
):
    width = fine.shape[-1]
    tokens = fine.shape[0] * fine.shape[1]
    flat = fine.reshape(tokens, width)
    coarse_flat = coarse.reshape(-1, coarse.shape[-1])
    keys = coarse_flat.shape[0]
    gain1 = attn_gain.reshape(1, width)
    gain2 = mlp_gain.reshape(1, width)
    smem = pl.BlockSpec(memory_space=pltpu.SMEM)
    anywhere = pl.BlockSpec(memory_space=pl.ANY)

    def room(like):
        return pltpu.VMEM(like.shape, like.dtype)

    operands = (
        flat,
        coarse_flat,
        gain1,
        w_query,
        w_key,
        w_value,
        w_out,
        coarse_key,
        coarse_value,
        gain2,
        w_gate,
        w_up,
        w_down,
    )
    flops = 2 * keys * coarse.shape[-1] * 2 * width + 6 * tokens * width * w_gate.shape[-1]
    result = pl.pallas_call(
        functools.partial(kernel, tiles, narrows),
        out_shape=jax.ShapeDtypeStruct((tokens, width), fine.dtype),
        in_specs=[smem, smem] + [anywhere] * len(operands),
        out_specs=pl.BlockSpec(memory_space=pltpu.VMEM),
        scratch_shapes=[
            pltpu.VMEM((3 * tokens, width), BF16),
            pltpu.VMEM((3 * tokens, width), BF16),
        ]
        + [room(x) for x in operands[1:]]
        + [
            pltpu.VMEM((keys, width), BF16),
            pltpu.VMEM((width, keys), BF16),
            pltpu.VMEM((width + 32, tokens), BF16),
            pltpu.VMEM((width + 16, tokens), BF16),
            pltpu.VMEM((width + 16, tokens), BF16),
            pltpu.VMEM((2, width, tokens), BF16),
            pltpu.VMEM((2, 2 * HEADS, tokens), F32),
            pltpu.VMEM((2, width, tokens), BF16),
            pltpu.VMEM((2, 2 * HEADS, tokens), F32),
            pltpu.VMEM((width, tokens), F32),
            pltpu.VMEM((2 * HEADS, tokens), F32),
            pltpu.SemaphoreType.DMA((len(operands),)),
            pltpu.SemaphoreType.DMA((12,)),
            pltpu.SemaphoreType.DMA((12,)),
        ],
        compiler_params=pltpu.CompilerParams(
            collective_id=0, has_side_effects=True, vmem_limit_bytes=48 * 1024 * 1024
        ),
        cost_estimate=pl.CostEstimate(
            flops=flops, bytes_accessed=12 * 1024 * 1024, transcendentals=2 * 1024 * 1024
        ),
    )(block_table, shifts, *operands)
    return result.reshape(fine.shape)


def solution(mesh):
    placed = (
        P("tile", "narrow", None),
        P("tile", None, None),
        P("tile", None),
    ) + (P(),) * 12
    return jax.shard_map(
        functools.partial(local, mesh.shape["tile"], mesh.shape["narrow"]),
        mesh=mesh,
        in_specs=placed,
        out_specs=P("tile", "narrow", None),
        check_vma=False,
    )
```

```python
import functools

import jax
import jax.numpy as jnp
from jax import lax
from jax.experimental import pallas as pl
from jax.experimental.pallas import tpu as pltpu
from jax.sharding import PartitionSpec as P

WS = 8
HD = 64
HEADS = 8
PAIR = 2 * HD
CT = 128
NB = 8
HIDDEN = -1e30
UNSEEN = -1e29
MESH = pl.DeviceIdType.MESH
F32 = jnp.float32
BF16 = jnp.bfloat16


def dot(a, b):
    return jnp.dot(a, b, preferred_element_type=F32)


def rms_scale(values, gain_vec):
    mean_square = jnp.mean(values * values, axis=-1, keepdims=True)
    return values * lax.rsqrt(mean_square + 1e-06) * gain_vec


def one_hot_rows(index, count):
    lanes = lax.broadcasted_iota(jnp.int32, (index.shape[0], count), 1)
    return (lanes == index).astype(F32).astype(BF16)


def paired(q_t):
    zero = jnp.zeros((HD, q_t.shape[1]), q_t.dtype)
    upper = jnp.concatenate([q_t[:HD], zero], axis=1)
    lower = jnp.concatenate([zero, q_t[HD:]], axis=1)
    return jnp.concatenate([upper, lower], axis=0)


def unpaired(both, tokens):
    return jnp.concatenate([both[:HD, :tokens], both[HD:, tokens:]], axis=0)


def kernel(
    tiles,
    narrows,
    table,
    shifts,
    fine,
    coarse,
    attn_gain,
    w_query,
    w_key,
    w_value,
    w_out,
    coarse_key,
    coarse_value,
    mlp_gain,
    w_gate,
    w_up,
    w_down,
    out,
    ext,
    far,
    coarse_v,
    gain1_v,
    wq_v,
    wk_v,
    wv_v,
    wo_v,
    ck_v,
    cv_v,
    gain2_v,
    wg_v,
    wu_v,
    wd_v,
    keys_v,
    values_t,
    table_send,
    table_recv,
    o_send,
    st_send,
    o_recv,
    st_recv,
    own_o,
    load_sem,
    send_sem,
    recv_sem,
):
    s = lax.axis_index("tile")
    n = lax.axis_index("narrow")
    s_next, s_prev = lax.rem(s + 1, tiles), lax.rem(s + tiles - 1, tiles)
    s_next2, s_prev2 = lax.rem(s + 2, tiles), lax.rem(s + tiles - 2, tiles)
    n_next, n_prev = lax.rem(n + 1, narrows), lax.rem(n + narrows - 1, narrows)
    tokens, width = fine.shape
    half = WS * WS
    rows_dev = tokens // WS
    blocks = coarse.shape[0] // CT
    two_sides = narrows > 2

    barrier = pltpu.get_barrier_semaphore()
    for peer in (
        (s_next, n),
        (s_prev, n),
        (s_next2, n),
        (s_prev2, n),
        (s, n_next),
        (s, n_prev),
    ):
        pl.semaphore_signal(barrier, inc=1, device_id=peer, device_id_type=MESH)

    pairs = (
        (coarse, coarse_v),
        (coarse_key, ck_v),
        (coarse_value, cv_v),
        (fine, ext.at[pl.ds(0, tokens)]),
        (attn_gain, gain1_v),
        (w_query, wq_v),
        (w_key, wk_v),
        (w_value, wv_v),
        (w_out, wo_v),
        (mlp_gain, gain2_v),
        (w_gate, wg_v),
        (w_up, wu_v),
        (w_down, wd_v),
    )
    loads = [
        pltpu.make_async_copy(src, dst, load_sem.at[i]) for i, (src, dst) in enumerate(pairs)
    ]
    for load in loads:
        load.start()

    def remote(slot, src, dst, peer):
        return pltpu.make_async_remote_copy(
            src_ref=src,
            dst_ref=dst,
            send_sem=send_sem.at[slot],
            recv_sem=recv_sem.at[slot],
            device_id=peer,
            device_id_type=MESH,
        )

    total = blocks * tiles
    entries = [
        lax.rem(table[0, i] - (s - 1) * blocks + total, total) for i in range(NB)
    ]

    def block_bias(j):
        hit = entries[0] == j
        for e in entries[1:]:
            hit = hit | (e == j)
        return jnp.where(hit, 0.0, HIDDEN).astype(F32)

    bias = [block_bias(j) for j in range(3 * blocks)]
    row = lax.broadcasted_iota(jnp.int32, (16, tokens), 0)
    filled = jnp.zeros((16, tokens), F32)
    for b in range(blocks):
        filled = jnp.where(row == b, bias[2 * blocks + b], filled)
        filled = jnp.where(row == 8 + b, bias[b], filled)
    table_send[...] = filled

    above, below, side, other = tokens, 2 * tokens, 3 * tokens, 5 * tokens
    pl.semaphore_wait(barrier, 6)
    table_copies = (
        remote(0, table_send.at[pl.ds(0, 8)], table_recv.at[0], (s_next, n)),
        remote(1, table_send.at[pl.ds(8, 8)], table_recv.at[1], (s_prev, n)),
    )
    to_prev = remote(2, fine, ext.at[pl.ds(below, tokens)], (s_prev, n))
    to_next = remote(3, fine, ext.at[pl.ds(above, tokens)], (s_next, n))
    to_far = remote(4, fine.at[pl.ds(0, half)], far, (s_prev2, n))
    sides = [remote(5, fine, ext.at[pl.ds(side, tokens)], (s, n_prev))]
    if two_sides:
        sides.append(remote(6, fine, ext.at[pl.ds(other, tokens)], (s, n_next)))
    for copy in (*table_copies, to_prev, to_next, to_far, *sides):
        copy.start()

    shift_row = shifts[0]
    shift_col = shifts[1]

    for i in range(3):
        loads[i].wait()
    keys_v[...] = dot(coarse_v[...], ck_v[...]).astype(BF16)
    values_t[...] = dot(coarse_v[...], cv_v[...]).T.astype(BF16)

    for i in range(3, 8):
        loads[i].wait()

    def normed_of(raw):
        return rms_scale(raw.astype(F32), gain1_v[...]).astype(BF16)

    def queries_of(raw):
        queries = dot(normed_of(raw), wq_v[...]) * (1.0 / HD**0.5)
        return queries.T.astype(BF16)

    for copy in table_copies:
        copy.wait()
    early = (lax.broadcasted_iota(jnp.int32, (1, tokens), 1) >> 3) < shift_row

    def token_bias(upper, lower):
        rows = []
        for x, y in zip(upper, lower):
            one = jnp.where(early, x, y)
            rows.append(jnp.concatenate([one, one], axis=1))
        return rows

    by_prev = [table_recv[0, pl.ds(b, 1), :] for b in range(blocks)]
    by_own = bias[blocks : 2 * blocks]
    by_next = [table_recv[1, pl.ds(b, 1), :] for b in range(blocks)]
    by_none = [HIDDEN] * blocks

    def attend(pair, q_t, biases):
        at = slice(pair * PAIR, (pair + 1) * PAIR)
        scores = dot(keys_v[:, at], paired(q_t[at]))
        parts = [scores[b * CT : (b + 1) * CT] for b in range(blocks)]
        top = None
        for part, hide in zip(parts, biases):
            high = jnp.max(part, axis=0, keepdims=True) + hide
            top = high if top is None else jnp.maximum(top, high)
        unseen = top < UNSEEN
        parts = [
            jnp.exp(part - jnp.where(unseen, -HIDDEN, top - hide))
            for part, hide in zip(parts, biases)
        ]
        amount = sum(jnp.sum(part, axis=0, keepdims=True) for part in parts)
        mixed = dot(values_t[at, :], jnp.concatenate(parts, axis=0).astype(BF16))
        return top, amount, unpaired(mixed, tokens)

    def split_heads(rows):
        halves = []
        for row in rows:
            halves += [row[:, :tokens], row[:, tokens:]]
        return jnp.concatenate(halves, axis=0)

    def cross(q_t, biases, store):
        tops, amounts = [], []
        for pair in range(HEADS // 2):
            top, amount, mixed = attend(pair, q_t, biases)
            store(pair, mixed)
            tops.append(top)
            amounts.append(amount)
        return split_heads(tops), split_heads(amounts)

    def neighbour(slot, raw, biases, peer):
        def store(pair, mixed):
            o_send[slot, pl.ds(pair * PAIR, PAIR), :] = mixed.astype(BF16)

        top, amount = cross(queries_of(raw), biases, store)
        st_send[slot, pl.ds(0, HEADS), :] = top
        st_send[slot, pl.ds(HEADS, HEADS), :] = amount
        copies = [
            remote(7 + 2 * slot, st_send.at[slot], st_recv.at[slot], peer),
            remote(8 + 2 * slot, o_send.at[slot], o_recv.at[slot], peer),
        ]
        for copy in copies:
            copy.start()
        return copies

    def keep(pair, mixed):
        own_o[0, pl.ds(pair * PAIR, PAIR), :] = mixed

    own = ext[pl.ds(0, tokens), :]
    own_q = queries_of(own)
    own_top, own_amount = cross(own_q, token_bias(by_prev, by_own), keep)

    forwards = []

    def forward(slot, at, place):
        src = ext.at[pl.ds(at, half)]
        copies = [remote(slot, src, ext.at[pl.ds(side + place, half)], (s, n_prev))]
        if two_sides:
            copies.append(
                remote(slot + 1, src, ext.at[pl.ds(other + place, half)], (s, n_next))
            )
        for copy in copies:
            copy.start()
        return copies

    to_prev.wait_recv()
    forwards += forward(13, below, tokens + half)
    part_copies = neighbour(
        0, ext[pl.ds(below, tokens), :], token_bias(by_own, by_next), (s_next, n)
    )
    to_next.wait_recv()
    forwards += forward(15, above + tokens - half, tokens)
    part_copies += neighbour(
        1, ext[pl.ds(above, tokens), :], token_bias(by_none, by_prev), (s_prev, n)
    )
    to_far.wait_recv()
    far_raw = far[...]
    part_copies += neighbour(
        2,
        jnp.concatenate([far_raw, far_raw], axis=0),
        token_bias(by_next, by_none),
        (s_next2, n),
    )

    for copy in sides:
        copy.wait_recv()
    for copy in forwards:
        copy.wait_recv()
    near = 6 * half
    k = lax.broadcasted_iota(jnp.int32, (near, 1), 0)
    row = (k >> 4) + shift_row - WS
    col = (k & 15) + shift_col - WS
    is_above, is_below = row < 0, row >= rows_dev
    is_left, is_right = col < 0, col >= WS
    row_in = jnp.where(is_above, row + rows_dev, jnp.where(is_below, row - rows_dev, row))
    col_in = jnp.where(is_left, col + WS, jnp.where(is_right, col - WS, col))
    middle = jnp.where(is_above, above, jnp.where(is_below, below, 0))
    beside = jnp.where(
        is_above, tokens - half, jnp.where(is_below, tokens + half, 0)
    ) + jnp.where(is_left, other if two_sides else side, side)
    place = jnp.where(is_left | is_right, beside, middle) + row_in * WS + col_in
    around = dot(one_hot_rows(place, ext.shape[0]), ext[...])
    normed = normed_of(around)
    keys_fine = dot(normed, wk_v[...]).astype(BF16)
    values_fine_t = dot(normed, wv_v[...]).T.astype(BF16)

    def label(row, col):
        g = s * rows_dev + row
        g = jnp.where(g < 0, g + rows_dev * tiles, g)
        g = jnp.where(g >= rows_dev * tiles, g - rows_dev * tiles, g)
        h = n * WS + col
        h = jnp.where(h < 0, h + WS * narrows, h)
        h = jnp.where(h >= WS * narrows, h - WS * narrows, h)
        window = ((row - shift_row + WS) >> 3) * 2 + ((col - shift_col + WS) >> 3)
        return window * 4 + jnp.where(g < shift_row, 2, 0) + jnp.where(h < shift_col, 1, 0)

    k = lax.broadcasted_iota(jnp.int32, (near, tokens), 0)
    t = lax.broadcasted_iota(jnp.int32, (near, tokens), 1)
    same = label((k >> 4) + shift_row - WS, (k & 15) + shift_col - WS) == label(t >> 3, t & 7)
    hide = jnp.where(same, 0.0, HIDDEN).astype(F32)
    hide = jnp.concatenate([hide, hide], axis=1)
    tops, amounts = [], []
    for pair in range(HEADS // 2):
        at = slice(pair * PAIR, (pair + 1) * PAIR)
        scores = dot(keys_fine[:, at], paired(own_q[at])) + hide
        top = jnp.max(scores, axis=0, keepdims=True)
        weights = jnp.exp(scores - top)
        tops.append(top)
        amounts.append(jnp.sum(weights, axis=0, keepdims=True))
        mixed = dot(values_fine_t[at, :], weights.astype(BF16))
        own_o[1, pl.ds(pair * PAIR, PAIR), :] = unpaired(mixed, tokens)
    self_top, self_amount = split_heads(tops), split_heads(amounts)

    for i in range(8, len(loads)):
        loads[i].wait()
    for copy in part_copies:
        copy.wait()
    for copy in (to_prev, to_next, to_far, *sides, *forwards):
        copy.wait_send()

    all_tops = [own_top, self_top] + [st_recv[i, pl.ds(0, HEADS), :] for i in range(3)]
    all_amounts = [own_amount, self_amount] + [
        st_recv[i, pl.ds(HEADS, HEADS), :] for i in range(3)
    ]
    top = functools.reduce(jnp.maximum, all_tops)
    scales = [jnp.exp(x - top) for x in all_tops]
    amount = sum(a * b for a, b in zip(scales, all_amounts))
    scales = [x / amount for x in scales]
    heads = []
    for h in range(HEADS):
        at = pl.ds(h * HD, HD)
        mixed = own_o[0, at, :] * scales[0][h : h + 1] + own_o[1, at, :] * scales[1][h : h + 1]
        for i in range(3):
            mixed = mixed + o_recv[i, at, :].astype(F32) * scales[2 + i][h : h + 1]
        heads.append(mixed)
    head_out = jnp.concatenate(heads, axis=0).T.astype(BF16)
    mid = ext[pl.ds(0, tokens), :].astype(F32) + dot(head_out, wo_v[...])
    normed_mid = rms_scale(mid, gain2_v[...]).astype(BF16)
    gate = dot(normed_mid, wg_v[...])
    up = dot(normed_mid, wu_v[...])
    hidden = (gate * lax.logistic(gate) * up).astype(BF16)
    out[...] = (mid + dot(hidden, wd_v[...])).astype(BF16)


def local(
    tiles,
    narrows,
    fine,
    coarse,
    block_table,
    shifts,
    attn_gain,
    w_query,
    w_key,
    w_value,
    w_out,
    coarse_key,
    coarse_value,
    mlp_gain,
    w_gate,
    w_up,
    w_down,
):
    width = fine.shape[-1]
    tokens = fine.shape[0] * fine.shape[1]
    flat = fine.reshape(tokens, width)
    coarse_flat = coarse.reshape(-1, coarse.shape[-1])
    keys = coarse_flat.shape[0]
    gain1 = attn_gain.reshape(1, width)
    gain2 = mlp_gain.reshape(1, width)
    smem = pl.BlockSpec(memory_space=pltpu.SMEM)
    anywhere = pl.BlockSpec(memory_space=pltpu.HBM)

    def room(like):
        return pltpu.VMEM(like.shape, like.dtype)

    operands = (
        flat,
        coarse_flat,
        gain1,
        w_query,
        w_key,
        w_value,
        w_out,
        coarse_key,
        coarse_value,
        gain2,
        w_gate,
        w_up,
        w_down,
    )
    flops = 2 * keys * coarse.shape[-1] * 2 * width + 6 * tokens * width * w_gate.shape[-1]
    result = pl.pallas_call(
        functools.partial(kernel, tiles, narrows),
        out_shape=jax.ShapeDtypeStruct((tokens, width), fine.dtype),
        in_specs=[smem, smem] + [anywhere] * len(operands),
        out_specs=pl.BlockSpec(memory_space=pltpu.VMEM),
        scratch_shapes=[
            pltpu.VMEM(((7 if narrows > 2 else 5) * tokens, width), BF16),
            pltpu.VMEM((WS * WS, width), BF16),
        ]
        + [room(x) for x in operands[1:]]
        + [
            pltpu.VMEM((keys, width), BF16),
            pltpu.VMEM((width, keys), BF16),
            pltpu.VMEM((16, tokens), F32),
            pltpu.VMEM((2, 8, tokens), F32),
            pltpu.VMEM((3, width, tokens), BF16),
            pltpu.VMEM((3, 2 * HEADS, tokens), F32),
            pltpu.VMEM((3, width, tokens), BF16),
            pltpu.VMEM((3, 2 * HEADS, tokens), F32),
            pltpu.VMEM((2, width, tokens), F32),
            pltpu.SemaphoreType.DMA((len(operands),)),
            pltpu.SemaphoreType.DMA((17,)),
            pltpu.SemaphoreType.DMA((17,)),
        ],
        compiler_params=pltpu.CompilerParams(
            collective_id=0, has_side_effects=True, vmem_limit_bytes=60 * 1024 * 1024
        ),
        cost_estimate=pl.CostEstimate(
            flops=flops, bytes_accessed=12 * 1024 * 1024, transcendentals=2 * 1024 * 1024
        ),
    )(block_table, shifts, *operands)
    return result.reshape(fine.shape)


def solution(mesh):
    placed = (
        P("tile", "narrow", None),
        P("tile", None, None),
        P("tile", None),
    ) + (P(),) * 12
    return jax.shard_map(
        functools.partial(local, mesh.shape["tile"], mesh.shape["narrow"]),
        mesh=mesh,
        in_specs=placed,
        out_specs=P("tile", "narrow", None),
        check_vma=False,
    )
```

```python
import functools

import jax
import jax.numpy as jnp
from jax import lax
from jax.experimental import pallas as pl
from jax.experimental.pallas import tpu as pltpu
from jax.sharding import PartitionSpec as P

WS = 8
HD = 64
HEADS = 8
PAIR = 2 * HD
CT = 128
NB = 8
HIDDEN = -1e30
UNSEEN = -1e29
MESH = pl.DeviceIdType.MESH
F32 = jnp.float32
BF16 = jnp.bfloat16


def dot(a, b):
    return jnp.dot(a, b, preferred_element_type=F32)


def rms_scale(values, gain_vec):
    mean_square = jnp.mean(values * values, axis=-1, keepdims=True)
    return values * lax.rsqrt(mean_square + 1e-06) * gain_vec


def one_hot_rows(index, count):
    lanes = lax.broadcasted_iota(jnp.int32, (index.shape[0], count), 1)
    return (lanes == index).astype(F32).astype(BF16)


def paired(q_t):
    zero = jnp.zeros((HD, q_t.shape[1]), q_t.dtype)
    upper = jnp.concatenate([q_t[:HD], zero], axis=1)
    lower = jnp.concatenate([zero, q_t[HD:]], axis=1)
    return jnp.concatenate([upper, lower], axis=0)


def unpaired(both, tokens):
    return jnp.concatenate([both[:HD, :tokens], both[HD:, tokens:]], axis=0)


def kernel(
    tiles,
    narrows,
    table,
    shifts,
    fine,
    coarse,
    attn_gain,
    w_query,
    w_key,
    w_value,
    w_out,
    coarse_key,
    coarse_value,
    mlp_gain,
    w_gate,
    w_up,
    w_down,
    out,
    ext,
    far,
    coarse_v,
    gain1_v,
    wq_v,
    wk_v,
    wv_v,
    wo_v,
    ck_v,
    cv_v,
    gain2_v,
    wg_v,
    wu_v,
    wd_v,
    keys_v,
    values_t,
    table_send,
    table_recv,
    o_send,
    st_send,
    o_recv,
    st_recv,
    own_o,
    load_sem,
    send_sem,
    recv_sem,
):
    s = lax.axis_index("tile")
    n = lax.axis_index("narrow")
    s_next, s_prev = lax.rem(s + 1, tiles), lax.rem(s + tiles - 1, tiles)
    s_next2, s_prev2 = lax.rem(s + 2, tiles), lax.rem(s + tiles - 2, tiles)
    n_next, n_prev = lax.rem(n + 1, narrows), lax.rem(n + narrows - 1, narrows)
    tokens, width = fine.shape
    half = WS * WS
    rows_dev = tokens // WS
    blocks = coarse.shape[0] // CT
    two_sides = narrows > 2

    barrier = pltpu.get_barrier_semaphore()
    for peer in (
        (s_next, n),
        (s_prev, n),
        (s_next2, n),
        (s_prev2, n),
        (s, n_next),
        (s, n_prev),
    ):
        pl.semaphore_signal(barrier, inc=1, device_id=peer, device_id_type=MESH)

    pairs = (
        (coarse, coarse_v),
        (coarse_key, ck_v),
        (coarse_value, cv_v),
        (fine, ext.at[pl.ds(0, tokens)]),
        (attn_gain, gain1_v),
        (w_query, wq_v),
        (w_key, wk_v),
        (w_value, wv_v),
        (w_out, wo_v),
        (mlp_gain, gain2_v),
        (w_gate, wg_v),
        (w_up, wu_v),
        (w_down, wd_v),
    )
    loads = [
        pltpu.make_async_copy(src, dst, load_sem.at[i]) for i, (src, dst) in enumerate(pairs)
    ]
    for load in loads:
        load.start()

    def remote(slot, src, dst, peer):
        return pltpu.make_async_remote_copy(
            src_ref=src,
            dst_ref=dst,
            send_sem=send_sem.at[slot],
            recv_sem=recv_sem.at[slot],
            device_id=peer,
            device_id_type=MESH,
        )

    total = blocks * tiles
    entries = [
        lax.rem(table[0, i] - (s - 1) * blocks + total, total) for i in range(NB)
    ]

    def block_bias(j):
        hit = entries[0] == j
        for e in entries[1:]:
            hit = hit | (e == j)
        return jnp.where(hit, 0.0, HIDDEN).astype(F32)

    bias = [block_bias(j) for j in range(3 * blocks)]
    row = lax.broadcasted_iota(jnp.int32, (16, tokens), 0)
    filled = jnp.zeros((16, tokens), F32)
    for b in range(blocks):
        filled = jnp.where(row == b, bias[2 * blocks + b], filled)
        filled = jnp.where(row == 8 + b, bias[b], filled)
    table_send[...] = filled

    above, below, side, other = tokens, 2 * tokens, 3 * tokens, 5 * tokens
    pl.semaphore_wait(barrier, 6)
    table_copies = (
        remote(0, table_send.at[pl.ds(0, 8)], table_recv.at[0], (s_next, n)),
        remote(1, table_send.at[pl.ds(8, 8)], table_recv.at[1], (s_prev, n)),
    )
    to_prev = remote(2, fine, ext.at[pl.ds(below, tokens)], (s_prev, n))
    to_next = remote(3, fine, ext.at[pl.ds(above, tokens)], (s_next, n))
    to_far = remote(4, fine.at[pl.ds(0, half)], far, (s_prev2, n))
    sides = [remote(5, fine, ext.at[pl.ds(side, tokens)], (s, n_prev))]
    if two_sides:
        sides.append(remote(6, fine, ext.at[pl.ds(other, tokens)], (s, n_next)))
    for copy in (*table_copies, to_far, to_prev, *sides):
        copy.start()

    shift_row = shifts[0]
    shift_col = shifts[1]

    for i in range(3):
        loads[i].wait()
    keys_v[...] = dot(coarse_v[...], ck_v[...]).astype(BF16)
    to_prev.wait_send()
    to_next.start()
    values_t[...] = dot(coarse_v[...], cv_v[...]).T.astype(BF16)

    for i in range(3, 8):
        loads[i].wait()

    def normed_of(raw):
        return rms_scale(raw.astype(F32), gain1_v[...]).astype(BF16)

    def queries_of(raw):
        queries = dot(normed_of(raw), wq_v[...]) * (1.0 / HD**0.5)
        return queries.T.astype(BF16)

    for copy in table_copies:
        copy.wait()
    early = (lax.broadcasted_iota(jnp.int32, (1, tokens), 1) >> 3) < shift_row

    def token_bias(upper, lower):
        rows = []
        for x, y in zip(upper, lower):
            one = jnp.where(early, x, y)
            rows.append(jnp.concatenate([one, one], axis=1))
        return rows

    by_prev = [table_recv[0, pl.ds(b, 1), :] for b in range(blocks)]
    by_own = bias[blocks : 2 * blocks]
    by_next = [table_recv[1, pl.ds(b, 1), :] for b in range(blocks)]
    by_none = [HIDDEN] * blocks

    def attend(pair, q_t, biases):
        at = slice(pair * PAIR, (pair + 1) * PAIR)
        scores = dot(keys_v[:, at], paired(q_t[at]))
        parts = [scores[b * CT : (b + 1) * CT] for b in range(blocks)]
        top = None
        for part, hide in zip(parts, biases):
            high = jnp.max(part, axis=0, keepdims=True) + hide
            top = high if top is None else jnp.maximum(top, high)
        unseen = top < UNSEEN
        parts = [
            jnp.exp(part - jnp.where(unseen, -HIDDEN, top - hide))
            for part, hide in zip(parts, biases)
        ]
        amount = sum(jnp.sum(part, axis=0, keepdims=True) for part in parts)
        mixed = dot(values_t[at, :], jnp.concatenate(parts, axis=0).astype(BF16))
        return top, amount, unpaired(mixed, tokens)

    def split_heads(rows):
        halves = []
        for row in rows:
            halves += [row[:, :tokens], row[:, tokens:]]
        return jnp.concatenate(halves, axis=0)

    def cross(q_t, biases, store):
        tops, amounts = [], []
        for pair in range(HEADS // 2):
            top, amount, mixed = attend(pair, q_t, biases)
            store(pair, mixed)
            tops.append(top)
            amounts.append(amount)
        return split_heads(tops), split_heads(amounts)

    def neighbour(slot, raw, biases, peer):
        def store(pair, mixed):
            o_send[slot, pl.ds(pair * PAIR, PAIR), :] = mixed.astype(BF16)

        top, amount = cross(queries_of(raw), biases, store)
        st_send[slot, pl.ds(0, HEADS), :] = top
        st_send[slot, pl.ds(HEADS, HEADS), :] = amount
        copies = [
            remote(7 + 2 * slot, st_send.at[slot], st_recv.at[slot], peer),
            remote(8 + 2 * slot, o_send.at[slot], o_recv.at[slot], peer),
        ]
        for copy in copies:
            copy.start()
        return copies

    def keep(pair, mixed):
        own_o[0, pl.ds(pair * PAIR, PAIR), :] = mixed

    forwards = []

    def forward(slot, at, place):
        src = ext.at[pl.ds(at, half)]
        copies = [remote(slot, src, ext.at[pl.ds(side + place, half)], (s, n_prev))]
        if two_sides:
            copies.append(
                remote(slot + 1, src, ext.at[pl.ds(other + place, half)], (s, n_next))
            )
        for copy in copies:
            copy.start()
        return copies

    to_far.wait_recv()
    far_raw = far[...]
    part_copies = neighbour(
        2,
        jnp.concatenate([far_raw, far_raw], axis=0),
        token_bias(by_next, by_none),
        (s_next2, n),
    )
    to_prev.wait_recv()
    forwards += forward(13, below, tokens + half)
    part_copies += neighbour(
        0, ext[pl.ds(below, tokens), :], token_bias(by_own, by_next), (s_next, n)
    )
    to_next.wait_recv()
    forwards += forward(15, above + tokens - half, tokens)
    part_copies += neighbour(
        1, ext[pl.ds(above, tokens), :], token_bias(by_none, by_prev), (s_prev, n)
    )

    own_q = queries_of(ext[pl.ds(0, tokens), :])
    own_top, own_amount = cross(own_q, token_bias(by_prev, by_own), keep)

    for copy in sides:
        copy.wait_recv()
    for copy in forwards:
        copy.wait_recv()
    near = 6 * half
    k = lax.broadcasted_iota(jnp.int32, (near, 1), 0)
    row = (k >> 4) + shift_row - WS
    col = (k & 15) + shift_col - WS
    is_above, is_below = row < 0, row >= rows_dev
    is_left, is_right = col < 0, col >= WS
    row_in = jnp.where(is_above, row + rows_dev, jnp.where(is_below, row - rows_dev, row))
    col_in = jnp.where(is_left, col + WS, jnp.where(is_right, col - WS, col))
    middle = jnp.where(is_above, above, jnp.where(is_below, below, 0))
    beside = jnp.where(
        is_above, tokens - half, jnp.where(is_below, tokens + half, 0)
    ) + jnp.where(is_left, other if two_sides else side, side)
    place = jnp.where(is_left | is_right, beside, middle) + row_in * WS + col_in
    around = dot(one_hot_rows(place, ext.shape[0]), ext[...])
    normed = normed_of(around)
    keys_fine = dot(normed, wk_v[...]).astype(BF16)
    values_fine_t = dot(normed, wv_v[...]).T.astype(BF16)

    def label(row, col):
        g = s * rows_dev + row
        g = jnp.where(g < 0, g + rows_dev * tiles, g)
        g = jnp.where(g >= rows_dev * tiles, g - rows_dev * tiles, g)
        h = n * WS + col
        h = jnp.where(h < 0, h + WS * narrows, h)
        h = jnp.where(h >= WS * narrows, h - WS * narrows, h)
        window = ((row - shift_row + WS) >> 3) * 2 + ((col - shift_col + WS) >> 3)
        return window * 4 + jnp.where(g < shift_row, 2, 0) + jnp.where(h < shift_col, 1, 0)

    k = lax.broadcasted_iota(jnp.int32, (near, tokens), 0)
    t = lax.broadcasted_iota(jnp.int32, (near, tokens), 1)
    same = label((k >> 4) + shift_row - WS, (k & 15) + shift_col - WS) == label(t >> 3, t & 7)
    hide = jnp.where(same, 0.0, HIDDEN).astype(F32)
    hide = jnp.concatenate([hide, hide], axis=1)
    tops, amounts = [], []
    for pair in range(HEADS // 2):
        at = slice(pair * PAIR, (pair + 1) * PAIR)
        scores = dot(keys_fine[:, at], paired(own_q[at])) + hide
        top = jnp.max(scores, axis=0, keepdims=True)
        weights = jnp.exp(scores - top)
        tops.append(top)
        amounts.append(jnp.sum(weights, axis=0, keepdims=True))
        mixed = dot(values_fine_t[at, :], weights.astype(BF16))
        own_o[1, pl.ds(pair * PAIR, PAIR), :] = unpaired(mixed, tokens)
    self_top, self_amount = split_heads(tops), split_heads(amounts)

    for i in range(8, len(loads)):
        loads[i].wait()
    for copy in part_copies:
        copy.wait()
    for copy in (to_next, to_far, *sides, *forwards):
        copy.wait_send()

    all_tops = [own_top, self_top] + [st_recv[i, pl.ds(0, HEADS), :] for i in range(3)]
    all_amounts = [own_amount, self_amount] + [
        st_recv[i, pl.ds(HEADS, HEADS), :] for i in range(3)
    ]
    top = functools.reduce(jnp.maximum, all_tops)
    scales = [jnp.exp(x - top) for x in all_tops]
    amount = sum(a * b for a, b in zip(scales, all_amounts))
    scales = [x / amount for x in scales]
    heads = []
    for h in range(HEADS):
        at = pl.ds(h * HD, HD)
        mixed = own_o[0, at, :] * scales[0][h : h + 1] + own_o[1, at, :] * scales[1][h : h + 1]
        for i in range(3):
            mixed = mixed + o_recv[i, at, :].astype(F32) * scales[2 + i][h : h + 1]
        heads.append(mixed)
    head_out = jnp.concatenate(heads, axis=0).T.astype(BF16)
    mid = ext[pl.ds(0, tokens), :].astype(F32) + dot(head_out, wo_v[...])
    normed_mid = rms_scale(mid, gain2_v[...]).astype(BF16)
    gate = dot(normed_mid, wg_v[...])
    up = dot(normed_mid, wu_v[...])
    hidden = (gate * lax.logistic(gate) * up).astype(BF16)
    out[...] = (mid + dot(hidden, wd_v[...])).astype(BF16)


def local(
    tiles,
    narrows,
    fine,
    coarse,
    block_table,
    shifts,
    attn_gain,
    w_query,
    w_key,
    w_value,
    w_out,
    coarse_key,
    coarse_value,
    mlp_gain,
    w_gate,
    w_up,
    w_down,
):
    width = fine.shape[-1]
    tokens = fine.shape[0] * fine.shape[1]
    flat = fine.reshape(tokens, width)
    coarse_flat = coarse.reshape(-1, coarse.shape[-1])
    keys = coarse_flat.shape[0]
    gain1 = attn_gain.reshape(1, width)
    gain2 = mlp_gain.reshape(1, width)
    smem = pl.BlockSpec(memory_space=pltpu.SMEM)
    anywhere = pl.BlockSpec(memory_space=pltpu.HBM)

    def room(like):
        return pltpu.VMEM(like.shape, like.dtype)

    operands = (
        flat,
        coarse_flat,
        gain1,
        w_query,
        w_key,
        w_value,
        w_out,
        coarse_key,
        coarse_value,
        gain2,
        w_gate,
        w_up,
        w_down,
    )
    flops = 2 * keys * coarse.shape[-1] * 2 * width + 6 * tokens * width * w_gate.shape[-1]
    result = pl.pallas_call(
        functools.partial(kernel, tiles, narrows),
        out_shape=jax.ShapeDtypeStruct((tokens, width), fine.dtype),
        in_specs=[smem, smem] + [anywhere] * len(operands),
        out_specs=pl.BlockSpec(memory_space=pltpu.VMEM),
        scratch_shapes=[
            pltpu.VMEM(((7 if narrows > 2 else 5) * tokens, width), BF16),
            pltpu.VMEM((WS * WS, width), BF16),
        ]
        + [room(x) for x in operands[1:]]
        + [
            pltpu.VMEM((keys, width), BF16),
            pltpu.VMEM((width, keys), BF16),
            pltpu.VMEM((16, tokens), F32),
            pltpu.VMEM((2, 8, tokens), F32),
            pltpu.VMEM((3, width, tokens), BF16),
            pltpu.VMEM((3, 2 * HEADS, tokens), F32),
            pltpu.VMEM((3, width, tokens), BF16),
            pltpu.VMEM((3, 2 * HEADS, tokens), F32),
            pltpu.VMEM((2, width, tokens), F32),
            pltpu.SemaphoreType.DMA((len(operands),)),
            pltpu.SemaphoreType.DMA((17,)),
            pltpu.SemaphoreType.DMA((17,)),
        ],
        compiler_params=pltpu.CompilerParams(
            collective_id=0, has_side_effects=True, vmem_limit_bytes=60 * 1024 * 1024
        ),
        cost_estimate=pl.CostEstimate(
            flops=flops, bytes_accessed=12 * 1024 * 1024, transcendentals=2 * 1024 * 1024
        ),
    )(block_table, shifts, *operands)
    return result.reshape(fine.shape)


def solution(mesh):
    placed = (
        P("tile", "narrow", None),
        P("tile", None, None),
        P("tile", None),
    ) + (P(),) * 12
    return jax.shard_map(
        functools.partial(local, mesh.shape["tile"], mesh.shape["narrow"]),
        mesh=mesh,
        in_specs=placed,
        out_specs=P("tile", "narrow", None),
        check_vma=False,
    )
```

```python
import functools

import jax
import jax.numpy as jnp
from jax import lax
from jax.experimental import pallas as pl
from jax.experimental.pallas import tpu as pltpu
from jax.sharding import PartitionSpec as P

WS = 8
HD = 64
HEADS = 8
PAIR = 2 * HD
CT = 128
NB = 8
HIDDEN = -1e30
UNSEEN = -1e29
MESH = pl.DeviceIdType.MESH
F32 = jnp.float32
BF16 = jnp.bfloat16


def dot(a, b):
    return jnp.dot(a, b, preferred_element_type=F32)


def rms_scale(values, gain_vec):
    mean_square = jnp.mean(values * values, axis=-1, keepdims=True)
    return values * lax.rsqrt(mean_square + 1e-06) * gain_vec


def one_hot_rows(index, count):
    lanes = lax.broadcasted_iota(jnp.int32, (index.shape[0], count), 1)
    return (lanes == index).astype(F32).astype(BF16)


def paired(q_t):
    zero = jnp.zeros((HD, q_t.shape[1]), q_t.dtype)
    upper = jnp.concatenate([q_t[:HD], zero], axis=1)
    lower = jnp.concatenate([zero, q_t[HD:]], axis=1)
    return jnp.concatenate([upper, lower], axis=0)


def unpaired(both, tokens):
    return jnp.concatenate([both[:HD, :tokens], both[HD:, tokens:]], axis=0)


def kernel(
    tiles,
    narrows,
    table_in,
    shifts_in,
    fine,
    coarse,
    attn_gain,
    w_query,
    w_key,
    w_value,
    w_out,
    coarse_key,
    coarse_value,
    mlp_gain,
    w_gate,
    w_up,
    w_down,
    out,
    ext,
    far,
    coarse_v,
    gain1_v,
    wq_v,
    wk_v,
    wv_v,
    wo_v,
    ck_v,
    cv_v,
    gain2_v,
    wg_v,
    wu_v,
    wd_v,
    keys_v,
    values_t,
    table_send,
    table_recv,
    o_send,
    st_send,
    o_recv,
    st_recv,
    own_o,
    table,
    shifts,
    load_sem,
    send_sem,
    recv_sem,
):
    s = lax.axis_index("tile")
    n = lax.axis_index("narrow")
    s_next, s_prev = lax.rem(s + 1, tiles), lax.rem(s + tiles - 1, tiles)
    s_next2, s_prev2 = lax.rem(s + 2, tiles), lax.rem(s + tiles - 2, tiles)
    n_next, n_prev = lax.rem(n + 1, narrows), lax.rem(n + narrows - 1, narrows)
    tokens, width = fine.shape
    half = WS * WS
    rows_dev = tokens // WS
    blocks = coarse.shape[0] // CT
    two_sides = narrows > 2

    barrier = pltpu.get_barrier_semaphore()
    for peer in (
        (s_next, n),
        (s_prev, n),
        (s_next2, n),
        (s_prev2, n),
        (s, n_next),
        (s, n_prev),
    ):
        pl.semaphore_signal(barrier, inc=1, device_id=peer, device_id_type=MESH)

    pairs = (
        (coarse, coarse_v),
        (coarse_key, ck_v),
        (coarse_value, cv_v),
        (table_in, table),
        (shifts_in, shifts),
        (fine, ext.at[pl.ds(0, tokens)]),
        (attn_gain, gain1_v),
        (w_query, wq_v),
        (w_key, wk_v),
        (w_value, wv_v),
        (w_out, wo_v),
        (mlp_gain, gain2_v),
        (w_gate, wg_v),
        (w_up, wu_v),
        (w_down, wd_v),
    )
    loads = [
        pltpu.make_async_copy(src, dst, load_sem.at[i]) for i, (src, dst) in enumerate(pairs)
    ]
    for i in (*range(3, 5), *range(3), *range(5, 8)):
        loads[i].start()

    def remote(slot, src, dst, peer):
        return pltpu.make_async_remote_copy(
            src_ref=src,
            dst_ref=dst,
            send_sem=send_sem.at[slot],
            recv_sem=recv_sem.at[slot],
            device_id=peer,
            device_id_type=MESH,
        )

    above, below, side, other = tokens, 2 * tokens, 3 * tokens, 5 * tokens
    pl.semaphore_wait(barrier, 6)
    to_prev = remote(2, fine, ext.at[pl.ds(below, tokens)], (s_prev, n))
    to_next = remote(3, fine, ext.at[pl.ds(above, tokens)], (s_next, n))
    to_far = remote(4, fine.at[pl.ds(0, half)], far, (s_prev2, n))
    sides = [remote(5, fine, ext.at[pl.ds(side, tokens)], (s, n_prev))]
    if two_sides:
        sides.append(remote(6, fine, ext.at[pl.ds(other, tokens)], (s, n_next)))
    for copy in (to_far, to_prev, *sides):
        copy.start()
    for i in range(8, len(loads)):
        loads[i].start()

    loads[3].wait()
    loads[4].wait()
    total = blocks * tiles
    entries = []
    for i in range(NB):
        e = table[0, i] - (s - 1) * blocks
        e = jnp.where(e < 0, e + total, e)
        entries.append(jnp.where(e >= total, e - total, e))

    def block_bias(j):
        hit = entries[0] == j
        for e in entries[1:]:
            hit = hit | (e == j)
        return jnp.where(hit, 0.0, HIDDEN).astype(F32)

    bias = [block_bias(j) for j in range(3 * blocks)]
    row = lax.broadcasted_iota(jnp.int32, (16, tokens), 0)
    filled = jnp.zeros((16, tokens), F32)
    for b in range(blocks):
        filled = jnp.where(row == b, bias[2 * blocks + b], filled)
        filled = jnp.where(row == 8 + b, bias[b], filled)
    table_send[...] = filled

    table_copies = (
        remote(0, table_send.at[pl.ds(0, 8)], table_recv.at[0], (s_next, n)),
        remote(1, table_send.at[pl.ds(8, 8)], table_recv.at[1], (s_prev, n)),
    )
    for copy in table_copies:
        copy.start()
    shift_row = shifts[0]
    shift_col = shifts[1]

    for i in range(3):
        loads[i].wait()
    keys_v[...] = dot(coarse_v[...], ck_v[...]).astype(BF16)
    values_t[...] = dot(coarse_v[...], cv_v[...]).T.astype(BF16)
    to_next.start()

    for i in range(5, 10):
        loads[i].wait()

    def normed_of(raw):
        return rms_scale(raw.astype(F32), gain1_v[...]).astype(BF16)

    def queries_of(raw):
        queries = dot(normed_of(raw), wq_v[...]) * (1.0 / HD**0.5)
        return queries.T.astype(BF16)

    for copy in table_copies:
        copy.wait()
    early = (lax.broadcasted_iota(jnp.int32, (1, tokens), 1) >> 3) < shift_row

    def token_bias(upper, lower):
        rows = []
        for x, y in zip(upper, lower):
            one = jnp.where(early, x, y)
            rows.append(jnp.concatenate([one, one], axis=1))
        return rows

    by_prev = [table_recv[0, pl.ds(b, 1), :] for b in range(blocks)]
    by_own = bias[blocks : 2 * blocks]
    by_next = [table_recv[1, pl.ds(b, 1), :] for b in range(blocks)]
    by_none = [HIDDEN] * blocks

    def attend(pair, q_t, biases):
        at = slice(pair * PAIR, (pair + 1) * PAIR)
        scores = dot(keys_v[:, at], paired(q_t[at]))
        parts = [scores[b * CT : (b + 1) * CT] for b in range(blocks)]
        top = None
        for part, hide in zip(parts, biases):
            high = jnp.max(part, axis=0, keepdims=True) + hide
            top = high if top is None else jnp.maximum(top, high)
        unseen = top < UNSEEN
        parts = [
            jnp.exp(part - jnp.where(unseen, -HIDDEN, top - hide))
            for part, hide in zip(parts, biases)
        ]
        amount = sum(jnp.sum(part, axis=0, keepdims=True) for part in parts)
        mixed = dot(values_t[at, :], jnp.concatenate(parts, axis=0).astype(BF16))
        return top, amount, unpaired(mixed, tokens)

    def split_heads(rows):
        halves = []
        for row in rows:
            halves += [row[:, :tokens], row[:, tokens:]]
        return jnp.concatenate(halves, axis=0)

    def cross(q_t, biases, store):
        tops, amounts = [], []
        for pair in range(HEADS // 2):
            top, amount, mixed = attend(pair, q_t, biases)
            store(pair, mixed)
            tops.append(top)
            amounts.append(amount)
        return split_heads(tops), split_heads(amounts)

    def neighbour(slot, raw, biases, peer):
        def store(pair, mixed):
            o_send[slot, pl.ds(pair * PAIR, PAIR), :] = mixed.astype(BF16)

        top, amount = cross(queries_of(raw), biases, store)
        st_send[slot, pl.ds(0, HEADS), :] = top
        st_send[slot, pl.ds(HEADS, HEADS), :] = amount
        copies = [
            remote(7 + 2 * slot, st_send.at[slot], st_recv.at[slot], peer),
            remote(8 + 2 * slot, o_send.at[slot], o_recv.at[slot], peer),
        ]
        for copy in copies:
            copy.start()
        return copies

    def keep(pair, mixed):
        own_o[0, pl.ds(pair * PAIR, PAIR), :] = mixed

    forwards = []

    def forward(slot, at, place):
        src = ext.at[pl.ds(at, half)]
        copies = [remote(slot, src, ext.at[pl.ds(side + place, half)], (s, n_prev))]
        if two_sides:
            copies.append(
                remote(slot + 1, src, ext.at[pl.ds(other + place, half)], (s, n_next))
            )
        for copy in copies:
            copy.start()
        return copies

    to_far.wait_recv()
    far_raw = far[...]
    part_copies = neighbour(
        2,
        jnp.concatenate([far_raw, far_raw], axis=0),
        token_bias(by_next, by_none),
        (s_next2, n),
    )
    to_prev.wait_recv()
    forwards += forward(13, below, tokens + half)
    part_copies += neighbour(
        0, ext[pl.ds(below, tokens), :], token_bias(by_own, by_next), (s_next, n)
    )
    to_next.wait_recv()
    forwards += forward(15, above + tokens - half, tokens)
    part_copies += neighbour(
        1, ext[pl.ds(above, tokens), :], token_bias(by_none, by_prev), (s_prev, n)
    )

    own_q = queries_of(ext[pl.ds(0, tokens), :])
    own_top, own_amount = cross(own_q, token_bias(by_prev, by_own), keep)

    for copy in sides:
        copy.wait_recv()
    for copy in forwards:
        copy.wait_recv()
    near = 6 * half
    k = lax.broadcasted_iota(jnp.int32, (near, 1), 0)
    row = (k >> 4) + shift_row - WS
    col = (k & 15) + shift_col - WS
    is_above, is_below = row < 0, row >= rows_dev
    is_left, is_right = col < 0, col >= WS
    row_in = jnp.where(is_above, row + rows_dev, jnp.where(is_below, row - rows_dev, row))
    col_in = jnp.where(is_left, col + WS, jnp.where(is_right, col - WS, col))
    middle = jnp.where(is_above, above, jnp.where(is_below, below, 0))
    beside = jnp.where(
        is_above, tokens - half, jnp.where(is_below, tokens + half, 0)
    ) + jnp.where(is_left, other if two_sides else side, side)
    place = jnp.where(is_left | is_right, beside, middle) + row_in * WS + col_in
    around = dot(one_hot_rows(place, ext.shape[0]), ext[...])
    normed = normed_of(around)
    keys_fine = dot(normed, wk_v[...]).astype(BF16)
    values_fine_t = dot(normed, wv_v[...]).T.astype(BF16)

    def label(row, col):
        g = s * rows_dev + row
        g = jnp.where(g < 0, g + rows_dev * tiles, g)
        g = jnp.where(g >= rows_dev * tiles, g - rows_dev * tiles, g)
        h = n * WS + col
        h = jnp.where(h < 0, h + WS * narrows, h)
        h = jnp.where(h >= WS * narrows, h - WS * narrows, h)
        window = ((row - shift_row + WS) >> 3) * 2 + ((col - shift_col + WS) >> 3)
        return window * 4 + jnp.where(g < shift_row, 2, 0) + jnp.where(h < shift_col, 1, 0)

    k = lax.broadcasted_iota(jnp.int32, (near, tokens), 0)
    t = lax.broadcasted_iota(jnp.int32, (near, tokens), 1)
    same = label((k >> 4) + shift_row - WS, (k & 15) + shift_col - WS) == label(t >> 3, t & 7)
    hide = jnp.where(same, 0.0, HIDDEN).astype(F32)
    hide = jnp.concatenate([hide, hide], axis=1)
    tops, amounts = [], []
    for pair in range(HEADS // 2):
        at = slice(pair * PAIR, (pair + 1) * PAIR)
        scores = dot(keys_fine[:, at], paired(own_q[at])) + hide
        top = jnp.max(scores, axis=0, keepdims=True)
        weights = jnp.exp(scores - top)
        tops.append(top)
        amounts.append(jnp.sum(weights, axis=0, keepdims=True))
        mixed = dot(values_fine_t[at, :], weights.astype(BF16))
        own_o[1, pl.ds(pair * PAIR, PAIR), :] = unpaired(mixed, tokens)
    self_top, self_amount = split_heads(tops), split_heads(amounts)

    for i in range(10, len(loads)):
        loads[i].wait()
    for copy in part_copies:
        copy.wait()
    for copy in (to_prev, to_next, to_far, *sides, *forwards):
        copy.wait_send()

    all_tops = [own_top, self_top] + [st_recv[i, pl.ds(0, HEADS), :] for i in range(3)]
    all_amounts = [own_amount, self_amount] + [
        st_recv[i, pl.ds(HEADS, HEADS), :] for i in range(3)
    ]
    top = functools.reduce(jnp.maximum, all_tops)
    scales = [jnp.exp(x - top) for x in all_tops]
    amount = sum(a * b for a, b in zip(scales, all_amounts))
    scales = [x / amount for x in scales]
    heads = []
    for h in range(HEADS):
        at = pl.ds(h * HD, HD)
        mixed = own_o[0, at, :] * scales[0][h : h + 1] + own_o[1, at, :] * scales[1][h : h + 1]
        for i in range(3):
            mixed = mixed + o_recv[i, at, :].astype(F32) * scales[2 + i][h : h + 1]
        heads.append(mixed)
    head_out = jnp.concatenate(heads, axis=0).T.astype(BF16)
    mid = ext[pl.ds(0, tokens), :].astype(F32) + dot(head_out, wo_v[...])
    normed_mid = rms_scale(mid, gain2_v[...]).astype(BF16)
    gate = dot(normed_mid, wg_v[...])
    up = dot(normed_mid, wu_v[...])
    hidden = (gate * lax.logistic(gate) * up).astype(BF16)
    out[...] = (mid + dot(hidden, wd_v[...])).astype(BF16)


def local(
    tiles,
    narrows,
    fine,
    coarse,
    block_table,
    shifts,
    attn_gain,
    w_query,
    w_key,
    w_value,
    w_out,
    coarse_key,
    coarse_value,
    mlp_gain,
    w_gate,
    w_up,
    w_down,
):
    width = fine.shape[-1]
    tokens = fine.shape[0] * fine.shape[1]
    flat = fine.reshape(tokens, width)
    coarse_flat = coarse.reshape(-1, coarse.shape[-1])
    keys = coarse_flat.shape[0]
    gain1 = attn_gain.reshape(1, width)
    gain2 = mlp_gain.reshape(1, width)
    anywhere = pl.BlockSpec(memory_space=pltpu.HBM)

    def room(like):
        return pltpu.VMEM(like.shape, like.dtype)

    small = tuple(
        pltpu.with_memory_space_constraint(x, pltpu.HBM) for x in (block_table, shifts)
    )
    operands = tuple(pltpu.with_memory_space_constraint(x, pltpu.HBM) for x in (
        flat,
        coarse_flat,
        gain1,
        w_query,
        w_key,
        w_value,
        w_out,
        coarse_key,
        coarse_value,
        gain2,
        w_gate,
        w_up,
        w_down,
    ))
    flops = 2 * keys * coarse.shape[-1] * 2 * width + 6 * tokens * width * w_gate.shape[-1]
    result = pl.pallas_call(
        functools.partial(kernel, tiles, narrows),
        out_shape=pltpu.VMEM((tokens, width), fine.dtype),
        in_specs=[anywhere] * (2 + len(operands)),
        out_specs=pl.BlockSpec(memory_space=pltpu.VMEM),
        scratch_shapes=[
            pltpu.VMEM(((7 if narrows > 2 else 5) * tokens, width), BF16),
            pltpu.VMEM((WS * WS, width), BF16),
        ]
        + [room(x) for x in operands[1:]]
        + [
            pltpu.VMEM((keys, width), BF16),
            pltpu.VMEM((width, keys), BF16),
            pltpu.VMEM((16, tokens), F32),
            pltpu.VMEM((2, 8, tokens), F32),
            pltpu.VMEM((3, width, tokens), BF16),
            pltpu.VMEM((3, 2 * HEADS, tokens), F32),
            pltpu.VMEM((3, width, tokens), BF16),
            pltpu.VMEM((3, 2 * HEADS, tokens), F32),
            pltpu.VMEM((2, width, tokens), F32),
            pltpu.SMEM(block_table.shape, jnp.int32),
            pltpu.SMEM(shifts.shape, jnp.int32),
            pltpu.SemaphoreType.DMA((2 + len(operands),)),
            pltpu.SemaphoreType.DMA((17,)),
            pltpu.SemaphoreType.DMA((17,)),
        ],
        compiler_params=pltpu.CompilerParams(
            collective_id=0, has_side_effects=True, vmem_limit_bytes=56 * 1024 * 1024
        ),
        cost_estimate=pl.CostEstimate(
            flops=flops, bytes_accessed=12 * 1024 * 1024, transcendentals=2 * 1024 * 1024
        ),
    )(*small, *operands)
    return result.reshape(fine.shape)


def solution(mesh):
    placed = (
        P("tile", "narrow", None),
        P("tile", None, None),
        P("tile", None),
    ) + (P(),) * 12
    return jax.shard_map(
        functools.partial(local, mesh.shape["tile"], mesh.shape["narrow"]),
        mesh=mesh,
        in_specs=placed,
        out_specs=P("tile", "narrow", None),
        check_vma=False,
    )
```

```python
import functools

import jax
import jax.numpy as jnp
from jax import lax
from jax.experimental import pallas as pl
from jax.experimental.pallas import tpu as pltpu
from jax.sharding import PartitionSpec as P

WS = 8
HD = 64
HEADS = 8
PAIR = 2 * HD
CT = 128
NB = 8
HIDDEN = -1e30
UNSEEN = -1e29
MESH = pl.DeviceIdType.MESH
F32 = jnp.float32
BF16 = jnp.bfloat16


def dot(a, b):
    return jnp.dot(a, b, preferred_element_type=F32)


def rms_scale(values, gain_vec):
    mean_square = jnp.mean(values * values, axis=-1, keepdims=True)
    return values * lax.rsqrt(mean_square + 1e-06) * gain_vec


def one_hot_rows(index, count):
    lanes = lax.broadcasted_iota(jnp.int32, (index.shape[0], count), 1)
    return (lanes == index).astype(F32).astype(BF16)


def paired(q_t):
    zero = jnp.zeros((HD, q_t.shape[1]), q_t.dtype)
    upper = jnp.concatenate([q_t[:HD], zero], axis=1)
    lower = jnp.concatenate([zero, q_t[HD:]], axis=1)
    return jnp.concatenate([upper, lower], axis=0)


def unpaired(both, tokens):
    return jnp.concatenate([both[:HD, :tokens], both[HD:, tokens:]], axis=0)


def kernel(
    tiles,
    narrows,
    table_in,
    shifts_in,
    fine,
    coarse,
    attn_gain,
    w_query,
    w_key,
    w_value,
    w_out,
    coarse_key,
    coarse_value,
    mlp_gain,
    w_gate,
    w_up,
    w_down,
    out,
    ext,
    far,
    coarse_v,
    gain1_v,
    wq_v,
    wk_v,
    wv_v,
    wo_v,
    ck_v,
    cv_v,
    gain2_v,
    wg_v,
    wu_v,
    wd_v,
    keys_v,
    values_t,
    table_send,
    table_recv,
    o_send,
    st_send,
    o_recv,
    st_recv,
    own_o,
    far_send,
    far_recv,
    far_st_send,
    far_st_recv,
    table,
    shifts,
    load_sem,
    send_sem,
    recv_sem,
):
    s = lax.axis_index("tile")
    n = lax.axis_index("narrow")
    s_next, s_prev = lax.rem(s + 1, tiles), lax.rem(s + tiles - 1, tiles)
    s_next2, s_prev2 = lax.rem(s + 2, tiles), lax.rem(s + tiles - 2, tiles)
    n_next, n_prev = lax.rem(n + 1, narrows), lax.rem(n + narrows - 1, narrows)
    tokens, width = fine.shape
    half = WS * WS
    rows_dev = tokens // WS
    blocks = coarse.shape[0] // CT
    two_sides = narrows > 2

    barrier = pltpu.get_barrier_semaphore()
    for peer in (
        (s_next, n),
        (s_prev, n),
        (s_next2, n),
        (s_prev2, n),
        (s, n_next),
        (s, n_prev),
    ):
        pl.semaphore_signal(barrier, inc=1, device_id=peer, device_id_type=MESH)

    pairs = (
        (coarse, coarse_v),
        (coarse_key, ck_v),
        (coarse_value, cv_v),
        (table_in, table),
        (shifts_in, shifts),
        (fine, ext.at[pl.ds(0, tokens)]),
        (attn_gain, gain1_v),
        (w_query, wq_v),
        (w_key, wk_v),
        (w_value, wv_v),
        (w_out, wo_v),
        (mlp_gain, gain2_v),
        (w_gate, wg_v),
        (w_up, wu_v),
        (w_down, wd_v),
    )
    loads = [
        pltpu.make_async_copy(src, dst, load_sem.at[i]) for i, (src, dst) in enumerate(pairs)
    ]
    for i in (*range(3, 5), *range(3), *range(5, 8)):
        loads[i].start()

    def remote(slot, src, dst, peer):
        return pltpu.make_async_remote_copy(
            src_ref=src,
            dst_ref=dst,
            send_sem=send_sem.at[slot],
            recv_sem=recv_sem.at[slot],
            device_id=peer,
            device_id_type=MESH,
        )

    above, below, side, other = tokens, 2 * tokens, 3 * tokens, 5 * tokens
    pl.semaphore_wait(barrier, 6)
    even = lax.rem(s, 2) == 0
    peer_a = jnp.where(even, s_prev, s_next)
    peer_b = jnp.where(even, s_next, s_prev)
    at_a = pl.multiple_of(jnp.where(even, above, below), half)
    at_b = pl.multiple_of(jnp.where(even, below, above), half)
    to_a = remote(2, fine, ext.at[pl.ds(at_b, tokens)], (peer_a, n))
    to_b = remote(3, fine, ext.at[pl.ds(at_a, tokens)], (peer_b, n))
    to_far = remote(4, fine.at[pl.ds(0, half)], far, (s_prev2, n))
    sides = [remote(5, fine, ext.at[pl.ds(side, tokens)], (s, n_prev))]
    if two_sides:
        sides.append(remote(6, fine, ext.at[pl.ds(other, tokens)], (s, n_next)))
    for copy in (to_far, to_a, *sides):
        copy.start()
    for i in range(8, len(loads)):
        loads[i].start()

    loads[3].wait()
    loads[4].wait()
    total = blocks * tiles
    entries = []
    for i in range(NB):
        e = table[0, i] - (s - 1) * blocks
        e = jnp.where(e < 0, e + total, e)
        entries.append(jnp.where(e >= total, e - total, e))

    def block_bias(j):
        hit = entries[0] == j
        for e in entries[1:]:
            hit = hit | (e == j)
        return jnp.where(hit, 0.0, HIDDEN).astype(F32)

    bias = [block_bias(j) for j in range(3 * blocks)]
    row = lax.broadcasted_iota(jnp.int32, (16, tokens), 0)
    filled = jnp.zeros((16, tokens), F32)
    for b in range(blocks):
        filled = jnp.where(row == b, bias[2 * blocks + b], filled)
        filled = jnp.where(row == 8 + b, bias[b], filled)
    table_send[...] = filled

    table_copies = (
        remote(0, table_send.at[pl.ds(0, 8)], table_recv.at[0], (s_next, n)),
        remote(1, table_send.at[pl.ds(8, 8)], table_recv.at[1], (s_prev, n)),
    )
    for copy in table_copies:
        copy.start()
    shift_row = shifts[0]
    shift_col = shifts[1]

    for i in range(3):
        loads[i].wait()
    keys_v[...] = dot(coarse_v[...], ck_v[...]).astype(BF16)
    values_t[...] = dot(coarse_v[...], cv_v[...]).T.astype(BF16)
    to_b.start()

    for i in range(5, 10):
        loads[i].wait()

    def normed_of(raw):
        return rms_scale(raw.astype(F32), gain1_v[...]).astype(BF16)

    def queries_of(raw):
        queries = dot(normed_of(raw), wq_v[...]) * (1.0 / HD**0.5)
        return queries.T.astype(BF16)

    for copy in table_copies:
        copy.wait()
    early = (lax.broadcasted_iota(jnp.int32, (1, tokens), 1) >> 3) < shift_row

    def token_bias(upper, lower):
        rows = []
        for x, y in zip(upper, lower):
            one = jnp.where(early, x, y)
            rows.append(jnp.concatenate([one, one], axis=1))
        return rows

    by_prev = [table_recv[0, pl.ds(b, 1), :] for b in range(blocks)]
    by_own = bias[blocks : 2 * blocks]
    by_next = [table_recv[1, pl.ds(b, 1), :] for b in range(blocks)]
    by_none = [HIDDEN] * blocks

    def attend(pair, q_pair, biases):
        at = slice(pair * PAIR, (pair + 1) * PAIR)
        scores = dot(keys_v[:, at], q_pair)
        parts = [scores[b * CT : (b + 1) * CT] for b in range(blocks)]
        top = None
        for part, hide in zip(parts, biases):
            high = jnp.max(part, axis=0, keepdims=True) + hide
            top = high if top is None else jnp.maximum(top, high)
        unseen = top < UNSEEN
        parts = [
            jnp.exp(part - jnp.where(unseen, -HIDDEN, top - hide))
            for part, hide in zip(parts, biases)
        ]
        amount = sum(jnp.sum(part, axis=0, keepdims=True) for part in parts)
        mixed = dot(values_t[at, :], jnp.concatenate(parts, axis=0).astype(BF16))
        return top, amount, mixed

    def split_heads(rows):
        halves = []
        for row in rows:
            halves += [row[:, :tokens], row[:, tokens:]]
        return jnp.concatenate(halves, axis=0)

    def cross(q_t, biases, store):
        tops, amounts = [], []
        for pair in range(HEADS // 2):
            q_pair = paired(q_t[pair * PAIR : (pair + 1) * PAIR])
            top, amount, mixed = attend(pair, q_pair, biases)
            store(pair, unpaired(mixed, tokens))
            tops.append(top)
            amounts.append(amount)
        return split_heads(tops), split_heads(amounts)

    def neighbour(slot, raw, biases, peer):
        def store(pair, mixed):
            o_send[slot, pl.ds(pair * PAIR, PAIR), :] = mixed.astype(BF16)

        top, amount = cross(queries_of(raw), biases, store)
        st_send[slot, pl.ds(0, HEADS), :] = top
        st_send[slot, pl.ds(HEADS, HEADS), :] = amount
        copies = [
            remote(7 + 2 * slot, st_send.at[slot], st_recv.at[slot], peer),
            remote(8 + 2 * slot, o_send.at[slot], o_recv.at[slot], peer),
        ]
        for copy in copies:
            copy.start()
        return copies

    def keep(pair, mixed):
        own_o[0, pl.ds(pair * PAIR, PAIR), :] = mixed

    forwards = []

    def forward(slot, at, place):
        src = ext.at[pl.ds(pl.multiple_of(at, half), half)]
        dst = ext.at[pl.ds(pl.multiple_of(side + place, half), half)]
        copies = [remote(slot, src, dst, (s, n_prev))]
        if two_sides:
            dst = ext.at[pl.ds(pl.multiple_of(other + place, half), half)]
            copies.append(remote(slot + 1, src, dst, (s, n_next)))
        for copy in copies:
            copy.start()
        return copies

    lane = lax.broadcasted_iota(jnp.int32, (1, tokens), 1)
    left_half = lane < half
    far_early = ((lane & (half - 1)) >> 3) < shift_row
    far_bias = [jnp.where(far_early, x, HIDDEN) for x in by_next]
    quadrant = (lax.broadcasted_iota(jnp.int32, (PAIR, tokens), 0) < HD) == (
        lax.broadcasted_iota(jnp.int32, (PAIR, tokens), 1) < half
    )
    quadrant = jnp.where(quadrant, 1.0, 0.0).astype(BF16)
    to_far.wait_recv()
    far_raw = far[...]
    far_q = queries_of(jnp.concatenate([far_raw, far_raw], axis=0))
    tops, amounts = [], []
    for pair in range(HEADS // 2):
        at = slice(pair * PAIR, (pair + 1) * PAIR)
        top, amount, mixed = attend(pair, far_q[at] * quadrant, far_bias)
        far_send[pl.ds(pair * HD, HD), :] = jnp.where(left_half, mixed[:HD], mixed[HD:]).astype(
            BF16
        )
        tops.append(top)
        amounts.append(amount)
    far_st_send[...] = jnp.concatenate(tops + amounts, axis=0)
    part_copies = [
        remote(11, far_st_send, far_st_recv, (s_next2, n)),
        remote(12, far_send, far_recv, (s_next2, n)),
    ]
    for copy in part_copies:
        copy.start()

    def choose(x, y):
        return [jnp.where(even, a, b) for a, b in zip(x, y)]

    last_above, first_below = above + tokens - half, below
    to_a.wait_recv()
    forwards += forward(
        13,
        jnp.where(even, last_above, first_below),
        jnp.where(even, tokens, tokens + half),
    )
    part_copies += neighbour(
        0,
        ext[pl.ds(at_a, tokens), :],
        token_bias(choose(by_none, by_own), choose(by_prev, by_next)),
        (peer_a, n),
    )
    to_b.wait_recv()
    forwards += forward(
        15,
        jnp.where(even, first_below, last_above),
        jnp.where(even, tokens + half, tokens),
    )
    part_copies += neighbour(
        1,
        ext[pl.ds(at_b, tokens), :],
        token_bias(choose(by_own, by_none), choose(by_next, by_prev)),
        (peer_b, n),
    )
    own_q = queries_of(ext[pl.ds(0, tokens), :])
    own_top, own_amount = cross(own_q, token_bias(by_prev, by_own), keep)

    for copy in sides:
        copy.wait_recv()
    for copy in forwards:
        copy.wait_recv()
    near = 6 * half
    k = lax.broadcasted_iota(jnp.int32, (near, 1), 0)
    row = (k >> 4) + shift_row - WS
    col = (k & 15) + shift_col - WS
    is_above, is_below = row < 0, row >= rows_dev
    is_left, is_right = col < 0, col >= WS
    row_in = jnp.where(is_above, row + rows_dev, jnp.where(is_below, row - rows_dev, row))
    col_in = jnp.where(is_left, col + WS, jnp.where(is_right, col - WS, col))
    middle = jnp.where(is_above, above, jnp.where(is_below, below, 0))
    beside = jnp.where(
        is_above, tokens - half, jnp.where(is_below, tokens + half, 0)
    ) + jnp.where(is_left, other if two_sides else side, side)
    place = jnp.where(is_left | is_right, beside, middle) + row_in * WS + col_in
    around = dot(one_hot_rows(place, ext.shape[0]), ext[...])
    normed = normed_of(around)
    keys_fine = dot(normed, wk_v[...]).astype(BF16)
    values_fine_t = dot(normed, wv_v[...]).T.astype(BF16)

    def label(row, col):
        g = s * rows_dev + row
        g = jnp.where(g < 0, g + rows_dev * tiles, g)
        g = jnp.where(g >= rows_dev * tiles, g - rows_dev * tiles, g)
        h = n * WS + col
        h = jnp.where(h < 0, h + WS * narrows, h)
        h = jnp.where(h >= WS * narrows, h - WS * narrows, h)
        window = ((row - shift_row + WS) >> 3) * 2 + ((col - shift_col + WS) >> 3)
        return window * 4 + jnp.where(g < shift_row, 2, 0) + jnp.where(h < shift_col, 1, 0)

    k = lax.broadcasted_iota(jnp.int32, (near, tokens), 0)
    t = lax.broadcasted_iota(jnp.int32, (near, tokens), 1)
    same = label((k >> 4) + shift_row - WS, (k & 15) + shift_col - WS) == label(t >> 3, t & 7)
    hide = jnp.where(same, 0.0, HIDDEN).astype(F32)
    hide = jnp.concatenate([hide, hide], axis=1)
    tops, amounts = [], []
    for pair in range(HEADS // 2):
        at = slice(pair * PAIR, (pair + 1) * PAIR)
        scores = dot(keys_fine[:, at], paired(own_q[at])) + hide
        top = jnp.max(scores, axis=0, keepdims=True)
        weights = jnp.exp(scores - top)
        tops.append(top)
        amounts.append(jnp.sum(weights, axis=0, keepdims=True))
        mixed = dot(values_fine_t[at, :], weights.astype(BF16))
        own_o[1, pl.ds(pair * PAIR, PAIR), :] = unpaired(mixed, tokens)
    self_top, self_amount = split_heads(tops), split_heads(amounts)

    for i in range(10, len(loads)):
        loads[i].wait()
    for copy in part_copies:
        copy.wait()
    for copy in (to_a, to_b, to_far, *sides, *forwards):
        copy.wait_send()

    def swapped(x):
        return jnp.concatenate([x[:, half:], x[:, :half]], axis=1)

    def far_rows(first, absent):
        straight = far_st_recv[pl.ds(first, HEADS // 2), :]
        crossed = swapped(straight)
        rows = []
        for i in range(HEADS // 2):
            rows += [straight[i : i + 1], crossed[i : i + 1]]
        return jnp.where(left_half, jnp.concatenate(rows, axis=0), absent)

    all_tops = [own_top, self_top] + [st_recv[i, pl.ds(0, HEADS), :] for i in range(2)]
    all_tops.append(far_rows(0, HIDDEN))
    all_amounts = [own_amount, self_amount] + [
        st_recv[i, pl.ds(HEADS, HEADS), :] for i in range(2)
    ]
    all_amounts.append(far_rows(HEADS // 2, 0.0))
    top = functools.reduce(jnp.maximum, all_tops)
    scales = [jnp.exp(x - top) for x in all_tops]
    amount = sum(a * b for a, b in zip(scales, all_amounts))
    scales = [x / amount for x in scales]
    heads = []
    for h in range(HEADS):
        at = pl.ds(h * HD, HD)
        mixed = own_o[0, at, :] * scales[0][h : h + 1] + own_o[1, at, :] * scales[1][h : h + 1]
        distant = far_recv[pl.ds(h // 2 * HD, HD), :].astype(F32)
        if h % 2:
            distant = swapped(distant)
        mixed = mixed + distant * scales[4][h : h + 1]
        for i in range(2):
            mixed = mixed + o_recv[i, at, :].astype(F32) * scales[2 + i][h : h + 1]
        heads.append(mixed)
    head_out = jnp.concatenate(heads, axis=0).T.astype(BF16)
    mid = ext[pl.ds(0, tokens), :].astype(F32) + dot(head_out, wo_v[...])
    normed_mid = rms_scale(mid, gain2_v[...]).astype(BF16)
    gate = dot(normed_mid, wg_v[...])
    up = dot(normed_mid, wu_v[...])
    hidden = (gate * lax.logistic(gate) * up).astype(BF16)
    out[...] = (mid + dot(hidden, wd_v[...])).astype(BF16)


def local(
    tiles,
    narrows,
    fine,
    coarse,
    block_table,
    shifts,
    attn_gain,
    w_query,
    w_key,
    w_value,
    w_out,
    coarse_key,
    coarse_value,
    mlp_gain,
    w_gate,
    w_up,
    w_down,
):
    width = fine.shape[-1]
    tokens = fine.shape[0] * fine.shape[1]
    flat = fine.reshape(tokens, width)
    coarse_flat = coarse.reshape(-1, coarse.shape[-1])
    keys = coarse_flat.shape[0]
    gain1 = attn_gain.reshape(1, width)
    gain2 = mlp_gain.reshape(1, width)
    anywhere = pl.BlockSpec(memory_space=pltpu.HBM)

    def room(like):
        return pltpu.VMEM(like.shape, like.dtype)

    small = tuple(
        pltpu.with_memory_space_constraint(x, pltpu.HBM) for x in (block_table, shifts)
    )
    operands = tuple(pltpu.with_memory_space_constraint(x, pltpu.HBM) for x in (
        flat,
        coarse_flat,
        gain1,
        w_query,
        w_key,
        w_value,
        w_out,
        coarse_key,
        coarse_value,
        gain2,
        w_gate,
        w_up,
        w_down,
    ))
    flops = 2 * keys * coarse.shape[-1] * 2 * width + 6 * tokens * width * w_gate.shape[-1]
    result = pl.pallas_call(
        functools.partial(kernel, tiles, narrows),
        out_shape=pltpu.VMEM((tokens, width), fine.dtype),
        in_specs=[anywhere] * (2 + len(operands)),
        out_specs=pl.BlockSpec(memory_space=pltpu.VMEM),
        scratch_shapes=[
            pltpu.VMEM(((7 if narrows > 2 else 5) * tokens, width), BF16),
            pltpu.VMEM((WS * WS, width), BF16),
        ]
        + [room(x) for x in operands[1:]]
        + [
            pltpu.VMEM((keys, width), BF16),
            pltpu.VMEM((width, keys), BF16),
            pltpu.VMEM((16, tokens), F32),
            pltpu.VMEM((2, 8, tokens), F32),
            pltpu.VMEM((2, width, tokens), BF16),
            pltpu.VMEM((2, 2 * HEADS, tokens), F32),
            pltpu.VMEM((2, width, tokens), BF16),
            pltpu.VMEM((2, 2 * HEADS, tokens), F32),
            pltpu.VMEM((2, width, tokens), F32),
            pltpu.VMEM((width // 2, tokens), BF16),
            pltpu.VMEM((width // 2, tokens), BF16),
            pltpu.VMEM((HEADS, tokens), F32),
            pltpu.VMEM((HEADS, tokens), F32),
            pltpu.SMEM(block_table.shape, jnp.int32),
            pltpu.SMEM(shifts.shape, jnp.int32),
            pltpu.SemaphoreType.DMA((2 + len(operands),)),
            pltpu.SemaphoreType.DMA((17,)),
            pltpu.SemaphoreType.DMA((17,)),
        ],
        compiler_params=pltpu.CompilerParams(
            collective_id=0, has_side_effects=True, vmem_limit_bytes=56 * 1024 * 1024
        ),
        cost_estimate=pl.CostEstimate(
            flops=flops, bytes_accessed=12 * 1024 * 1024, transcendentals=2 * 1024 * 1024
        ),
    )(*small, *operands)
    return result.reshape(fine.shape)


def solution(mesh):
    placed = (
        P("tile", "narrow", None),
        P("tile", None, None),
        P("tile", None),
    ) + (P(),) * 12
    return jax.shard_map(
        functools.partial(local, mesh.shape["tile"], mesh.shape["narrow"]),
        mesh=mesh,
        in_specs=placed,
        out_specs=P("tile", "narrow", None),
        check_vma=False,
    )
```

```python
import functools

import jax
import jax.numpy as jnp
from jax import lax
from jax.experimental import pallas as pl
from jax.experimental.pallas import tpu as pltpu
from jax.sharding import PartitionSpec as P

WS = 8
HD = 64
HEADS = 8
PAIR = 2 * HD
CT = 128
NB = 8
HIDDEN = -1e30
UNSEEN = -1e29
MESH = pl.DeviceIdType.MESH
F32 = jnp.float32
BF16 = jnp.bfloat16


def dot(a, b):
    return jnp.dot(a, b, preferred_element_type=F32)


def rms_scale(values, gain_vec):
    mean_square = jnp.mean(values * values, axis=-1, keepdims=True)
    return values * lax.rsqrt(mean_square + 1e-06) * gain_vec


def one_hot_rows(index, count):
    lanes = lax.broadcasted_iota(jnp.int32, (index.shape[0], count), 1)
    return (lanes == index).astype(F32).astype(BF16)


def paired(q_t):
    zero = jnp.zeros((HD, q_t.shape[1]), q_t.dtype)
    upper = jnp.concatenate([q_t[:HD], zero], axis=1)
    lower = jnp.concatenate([zero, q_t[HD:]], axis=1)
    return jnp.concatenate([upper, lower], axis=0)


def unpaired(both, tokens):
    return jnp.concatenate([both[:HD, :tokens], both[HD:, tokens:]], axis=0)


def kernel(
    tiles,
    narrows,
    table_in,
    shifts_in,
    fine,
    coarse,
    attn_gain,
    w_query,
    w_key,
    w_value,
    w_out,
    coarse_key,
    coarse_value,
    mlp_gain,
    w_gate,
    w_up,
    w_down,
    out,
    ext,
    far,
    coarse_v,
    gain1_v,
    wq_v,
    wk_v,
    wv_v,
    wo_v,
    ck_v,
    cv_v,
    gain2_v,
    wg_v,
    wu_v,
    wd_v,
    keys_v,
    values_t,
    table_send,
    table_recv,
    o_send,
    st_send,
    o_recv,
    st_recv,
    own_o,
    far_send,
    far_recv,
    far_st_send,
    far_st_recv,
    table,
    shifts,
    load_sem,
    send_sem,
    recv_sem,
):
    s = lax.axis_index("tile")
    n = lax.axis_index("narrow")
    s_next, s_prev = lax.rem(s + 1, tiles), lax.rem(s + tiles - 1, tiles)
    s_next2, s_prev2 = lax.rem(s + 2, tiles), lax.rem(s + tiles - 2, tiles)
    n_next, n_prev = lax.rem(n + 1, narrows), lax.rem(n + narrows - 1, narrows)
    tokens, width = fine.shape
    half = WS * WS
    rows_dev = tokens // WS
    blocks = coarse.shape[0] // CT
    two_sides = narrows > 2

    barrier = pltpu.get_barrier_semaphore()
    for peer in (
        (s_next, n),
        (s_prev, n),
        (s_next2, n),
        (s_prev2, n),
        (s, n_next),
        (s, n_prev),
    ):
        pl.semaphore_signal(barrier, inc=1, device_id=peer, device_id_type=MESH)

    pairs = (
        (coarse, coarse_v),
        (coarse_key, ck_v),
        (coarse_value, cv_v),
        (table_in, table),
        (shifts_in, shifts),
        (fine, ext.at[pl.ds(0, tokens)]),
        (attn_gain, gain1_v),
        (w_query, wq_v),
        (w_key, wk_v),
        (w_value, wv_v),
        (w_out, wo_v),
        (mlp_gain, gain2_v),
        (w_gate, wg_v),
        (w_up, wu_v),
        (w_down, wd_v),
    )
    loads = [
        pltpu.make_async_copy(src, dst, load_sem.at[i]) for i, (src, dst) in enumerate(pairs)
    ]
    for i in (*range(3, 5), *range(3), *range(5, 8)):
        loads[i].start()

    def remote(slot, src, dst, peer):
        return pltpu.make_async_remote_copy(
            src_ref=src,
            dst_ref=dst,
            send_sem=send_sem.at[slot],
            recv_sem=recv_sem.at[slot],
            device_id=peer,
            device_id_type=MESH,
        )

    above, below, side, other = tokens, 2 * tokens, 3 * tokens, 5 * tokens
    pl.semaphore_wait(barrier, 6)
    even = lax.rem(s, 2) == 0
    peer_a = jnp.where(even, s_prev, s_next)
    peer_b = jnp.where(even, s_next, s_prev)
    at_a = pl.multiple_of(jnp.where(even, above, below), half)
    at_b = pl.multiple_of(jnp.where(even, below, above), half)
    to_a = remote(2, fine, ext.at[pl.ds(at_b, tokens)], (peer_a, n))
    to_b = remote(3, fine, ext.at[pl.ds(at_a, tokens)], (peer_b, n))
    to_far = remote(4, fine.at[pl.ds(0, half)], far, (s_prev2, n))
    sides = [remote(5, fine, ext.at[pl.ds(side, tokens)], (s, n_prev))]
    if two_sides:
        sides.append(remote(6, fine, ext.at[pl.ds(other, tokens)], (s, n_next)))
    for copy in (to_a, to_far, *sides):
        copy.start()
    for i in range(8, len(loads)):
        loads[i].start()

    loads[3].wait()
    loads[4].wait()
    total = blocks * tiles
    entries = []
    for i in range(NB):
        e = table[0, i] - (s - 1) * blocks
        e = jnp.where(e < 0, e + total, e)
        entries.append(jnp.where(e >= total, e - total, e))

    def block_bias(j):
        hit = entries[0] == j
        for e in entries[1:]:
            hit = hit | (e == j)
        return jnp.where(hit, 0.0, HIDDEN).astype(F32)

    bias = [block_bias(j) for j in range(3 * blocks)]
    row = lax.broadcasted_iota(jnp.int32, (16, tokens), 0)
    filled = jnp.zeros((16, tokens), F32)
    for b in range(blocks):
        filled = jnp.where(row == b, bias[2 * blocks + b], filled)
        filled = jnp.where(row == 8 + b, bias[b], filled)
    table_send[...] = filled

    table_copies = (
        remote(0, table_send.at[pl.ds(0, 8)], table_recv.at[0], (s_next, n)),
        remote(1, table_send.at[pl.ds(8, 8)], table_recv.at[1], (s_prev, n)),
    )
    for copy in table_copies:
        copy.start()
    shift_row = shifts[0]
    shift_col = shifts[1]

    for i in range(3):
        loads[i].wait()
    keys_v[...] = dot(coarse_v[...], ck_v[...]).astype(BF16)
    values_t[...] = dot(coarse_v[...], cv_v[...]).T.astype(BF16)
    to_b.start()

    for i in range(5, 10):
        loads[i].wait()

    def normed_of(raw):
        return rms_scale(raw.astype(F32), gain1_v[...]).astype(BF16)

    def queries_of(raw):
        queries = dot(normed_of(raw), wq_v[...]) * (1.0 / HD**0.5)
        return queries.T.astype(BF16)

    for copy in table_copies:
        copy.wait()
    early = (lax.broadcasted_iota(jnp.int32, (1, tokens), 1) >> 3) < shift_row

    def token_bias(upper, lower):
        rows = []
        for x, y in zip(upper, lower):
            one = jnp.where(early, x, y)
            rows.append(jnp.concatenate([one, one], axis=1))
        return rows

    by_prev = [table_recv[0, pl.ds(b, 1), :] for b in range(blocks)]
    by_own = bias[blocks : 2 * blocks]
    by_next = [table_recv[1, pl.ds(b, 1), :] for b in range(blocks)]
    by_none = [HIDDEN] * blocks

    def attend(pair, q_pair, biases):
        at = slice(pair * PAIR, (pair + 1) * PAIR)
        scores = dot(keys_v[:, at], q_pair)
        parts = [scores[b * CT : (b + 1) * CT] for b in range(blocks)]
        top = None
        for part, hide in zip(parts, biases):
            high = jnp.max(part, axis=0, keepdims=True) + hide
            top = high if top is None else jnp.maximum(top, high)
        unseen = top < UNSEEN
        parts = [
            jnp.exp(part - jnp.where(unseen, -HIDDEN, top - hide))
            for part, hide in zip(parts, biases)
        ]
        amount = sum(jnp.sum(part, axis=0, keepdims=True) for part in parts)
        mixed = dot(values_t[at, :], jnp.concatenate(parts, axis=0).astype(BF16))
        return top, amount, mixed

    def split_heads(rows):
        halves = []
        for row in rows:
            halves += [row[:, :tokens], row[:, tokens:]]
        return jnp.concatenate(halves, axis=0)

    def cross(q_t, biases, store):
        tops, amounts = [], []
        for pair in range(HEADS // 2):
            q_pair = paired(q_t[pair * PAIR : (pair + 1) * PAIR])
            top, amount, mixed = attend(pair, q_pair, biases)
            store(pair, unpaired(mixed, tokens))
            tops.append(top)
            amounts.append(amount)
        return split_heads(tops), split_heads(amounts)

    def neighbour(slot, raw, biases, peer):
        def store(pair, mixed):
            o_send[slot, pl.ds(pair * PAIR, PAIR), :] = mixed.astype(BF16)

        top, amount = cross(queries_of(raw), biases, store)
        st_send[slot, pl.ds(0, HEADS), :] = top
        st_send[slot, pl.ds(HEADS, HEADS), :] = amount
        copies = [
            remote(7 + 2 * slot, st_send.at[slot], st_recv.at[slot], peer),
            remote(8 + 2 * slot, o_send.at[slot], o_recv.at[slot], peer),
        ]
        for copy in copies:
            copy.start()
        return copies

    def keep(pair, mixed):
        own_o[0, pl.ds(pair * PAIR, PAIR), :] = mixed

    forwards = []

    def forward(slot, at, place):
        src = ext.at[pl.ds(pl.multiple_of(at, half), half)]
        dst = ext.at[pl.ds(pl.multiple_of(side + place, half), half)]
        copies = [remote(slot, src, dst, (s, n_prev))]
        if two_sides:
            dst = ext.at[pl.ds(pl.multiple_of(other + place, half), half)]
            copies.append(remote(slot + 1, src, dst, (s, n_next)))
        for copy in copies:
            copy.start()
        return copies

    own_q = queries_of(ext[pl.ds(0, tokens), :])
    own_top, own_amount = cross(own_q, token_bias(by_prev, by_own), keep)

    def choose(x, y):
        return [jnp.where(even, a, b) for a, b in zip(x, y)]

    last_above, first_below = above + tokens - half, below
    to_a.wait_recv()
    forwards += forward(
        13,
        jnp.where(even, last_above, first_below),
        jnp.where(even, tokens, tokens + half),
    )
    part_copies = neighbour(
        0,
        ext[pl.ds(at_a, tokens), :],
        token_bias(choose(by_none, by_own), choose(by_prev, by_next)),
        (peer_a, n),
    )
    to_b.wait_recv()
    forwards += forward(
        15,
        jnp.where(even, first_below, last_above),
        jnp.where(even, tokens + half, tokens),
    )
    part_copies += neighbour(
        1,
        ext[pl.ds(at_b, tokens), :],
        token_bias(choose(by_own, by_none), choose(by_next, by_prev)),
        (peer_b, n),
    )
    lane = lax.broadcasted_iota(jnp.int32, (1, tokens), 1)
    left_half = lane < half
    far_early = ((lane & (half - 1)) >> 3) < shift_row
    far_bias = [jnp.where(far_early, x, HIDDEN) for x in by_next]
    quadrant = (lax.broadcasted_iota(jnp.int32, (PAIR, tokens), 0) < HD) == (
        lax.broadcasted_iota(jnp.int32, (PAIR, tokens), 1) < half
    )
    quadrant = jnp.where(quadrant, 1.0, 0.0).astype(BF16)
    to_far.wait_recv()
    far_raw = far[...]
    far_q = queries_of(jnp.concatenate([far_raw, far_raw], axis=0))
    tops, amounts = [], []
    for pair in range(HEADS // 2):
        at = slice(pair * PAIR, (pair + 1) * PAIR)
        top, amount, mixed = attend(pair, far_q[at] * quadrant, far_bias)
        far_send[pl.ds(pair * HD, HD), :] = jnp.where(left_half, mixed[:HD], mixed[HD:]).astype(
            BF16
        )
        tops.append(top)
        amounts.append(amount)
    far_st_send[...] = jnp.concatenate(tops + amounts, axis=0)
    far_copies = [
        remote(11, far_st_send, far_st_recv, (s_next2, n)),
        remote(12, far_send, far_recv, (s_next2, n)),
    ]
    for copy in far_copies:
        copy.start()
    part_copies += far_copies

    for copy in sides:
        copy.wait_recv()
    for copy in forwards:
        copy.wait_recv()
    near = 6 * half
    k = lax.broadcasted_iota(jnp.int32, (near, 1), 0)
    row = (k >> 4) + shift_row - WS
    col = (k & 15) + shift_col - WS
    is_above, is_below = row < 0, row >= rows_dev
    is_left, is_right = col < 0, col >= WS
    row_in = jnp.where(is_above, row + rows_dev, jnp.where(is_below, row - rows_dev, row))
    col_in = jnp.where(is_left, col + WS, jnp.where(is_right, col - WS, col))
    middle = jnp.where(is_above, above, jnp.where(is_below, below, 0))
    beside = jnp.where(
        is_above, tokens - half, jnp.where(is_below, tokens + half, 0)
    ) + jnp.where(is_left, other if two_sides else side, side)
    place = jnp.where(is_left | is_right, beside, middle) + row_in * WS + col_in
    around = dot(one_hot_rows(place, ext.shape[0]), ext[...])
    normed = normed_of(around)
    keys_fine = dot(normed, wk_v[...]).astype(BF16)
    values_fine_t = dot(normed, wv_v[...]).T.astype(BF16)

    def label(row, col):
        g = s * rows_dev + row
        g = jnp.where(g < 0, g + rows_dev * tiles, g)
        g = jnp.where(g >= rows_dev * tiles, g - rows_dev * tiles, g)
        h = n * WS + col
        h = jnp.where(h < 0, h + WS * narrows, h)
        h = jnp.where(h >= WS * narrows, h - WS * narrows, h)
        window = ((row - shift_row + WS) >> 3) * 2 + ((col - shift_col + WS) >> 3)
        return window * 4 + jnp.where(g < shift_row, 2, 0) + jnp.where(h < shift_col, 1, 0)

    k = lax.broadcasted_iota(jnp.int32, (near, tokens), 0)
    t = lax.broadcasted_iota(jnp.int32, (near, tokens), 1)
    same = label((k >> 4) + shift_row - WS, (k & 15) + shift_col - WS) == label(t >> 3, t & 7)
    hide = jnp.where(same, 0.0, HIDDEN).astype(F32)
    hide = jnp.concatenate([hide, hide], axis=1)
    tops, amounts = [], []
    for pair in range(HEADS // 2):
        at = slice(pair * PAIR, (pair + 1) * PAIR)
        scores = dot(keys_fine[:, at], paired(own_q[at])) + hide
        top = jnp.max(scores, axis=0, keepdims=True)
        weights = jnp.exp(scores - top)
        tops.append(top)
        amounts.append(jnp.sum(weights, axis=0, keepdims=True))
        mixed = dot(values_fine_t[at, :], weights.astype(BF16))
        own_o[1, pl.ds(pair * PAIR, PAIR), :] = unpaired(mixed, tokens)
    self_top, self_amount = split_heads(tops), split_heads(amounts)

    for i in range(10, len(loads)):
        loads[i].wait()
    for copy in part_copies:
        copy.wait()
    for copy in (to_a, to_b, to_far, *sides, *forwards):
        copy.wait_send()

    def swapped(x):
        return jnp.concatenate([x[:, half:], x[:, :half]], axis=1)

    def far_rows(first, absent):
        straight = far_st_recv[pl.ds(first, HEADS // 2), :]
        crossed = swapped(straight)
        rows = []
        for i in range(HEADS // 2):
            rows += [straight[i : i + 1], crossed[i : i + 1]]
        return jnp.where(left_half, jnp.concatenate(rows, axis=0), absent)

    all_tops = [own_top, self_top] + [st_recv[i, pl.ds(0, HEADS), :] for i in range(2)]
    all_tops.append(far_rows(0, HIDDEN))
    all_amounts = [own_amount, self_amount] + [
        st_recv[i, pl.ds(HEADS, HEADS), :] for i in range(2)
    ]
    all_amounts.append(far_rows(HEADS // 2, 0.0))
    top = functools.reduce(jnp.maximum, all_tops)
    scales = [jnp.exp(x - top) for x in all_tops]
    amount = sum(a * b for a, b in zip(scales, all_amounts))
    scales = [x / amount for x in scales]
    heads = []
    for h in range(HEADS):
        at = pl.ds(h * HD, HD)
        mixed = own_o[0, at, :] * scales[0][h : h + 1] + own_o[1, at, :] * scales[1][h : h + 1]
        distant = far_recv[pl.ds(h // 2 * HD, HD), :].astype(F32)
        if h % 2:
            distant = swapped(distant)
        mixed = mixed + distant * scales[4][h : h + 1]
        for i in range(2):
            mixed = mixed + o_recv[i, at, :].astype(F32) * scales[2 + i][h : h + 1]
        heads.append(mixed)
    head_out = jnp.concatenate(heads, axis=0).T.astype(BF16)
    mid = ext[pl.ds(0, tokens), :].astype(F32) + dot(head_out, wo_v[...])
    normed_mid = rms_scale(mid, gain2_v[...]).astype(BF16)
    gate = dot(normed_mid, wg_v[...])
    up = dot(normed_mid, wu_v[...])
    hidden = (gate * lax.logistic(gate) * up).astype(BF16)
    out[...] = (mid + dot(hidden, wd_v[...])).astype(BF16)


def local(
    tiles,
    narrows,
    fine,
    coarse,
    block_table,
    shifts,
    attn_gain,
    w_query,
    w_key,
    w_value,
    w_out,
    coarse_key,
    coarse_value,
    mlp_gain,
    w_gate,
    w_up,
    w_down,
):
    width = fine.shape[-1]
    tokens = fine.shape[0] * fine.shape[1]
    flat = fine.reshape(tokens, width)
    coarse_flat = coarse.reshape(-1, coarse.shape[-1])
    keys = coarse_flat.shape[0]
    gain1 = attn_gain.reshape(1, width)
    gain2 = mlp_gain.reshape(1, width)
    anywhere = pl.BlockSpec(memory_space=pltpu.HBM)

    def room(like):
        return pltpu.VMEM(like.shape, like.dtype)

    small = tuple(
        pltpu.with_memory_space_constraint(x, pltpu.HBM) for x in (block_table, shifts)
    )
    operands = tuple(pltpu.with_memory_space_constraint(x, pltpu.HBM) for x in (
        flat,
        coarse_flat,
        gain1,
        w_query,
        w_key,
        w_value,
        w_out,
        coarse_key,
        coarse_value,
        gain2,
        w_gate,
        w_up,
        w_down,
    ))
    flops = 2 * keys * coarse.shape[-1] * 2 * width + 6 * tokens * width * w_gate.shape[-1]
    result = pl.pallas_call(
        functools.partial(kernel, tiles, narrows),
        out_shape=pltpu.VMEM((tokens, width), fine.dtype),
        in_specs=[anywhere] * (2 + len(operands)),
        out_specs=pl.BlockSpec(memory_space=pltpu.VMEM),
        scratch_shapes=[
            pltpu.VMEM(((7 if narrows > 2 else 5) * tokens, width), BF16),
            pltpu.VMEM((WS * WS, width), BF16),
        ]
        + [room(x) for x in operands[1:]]
        + [
            pltpu.VMEM((keys, width), BF16),
            pltpu.VMEM((width, keys), BF16),
            pltpu.VMEM((16, tokens), F32),
            pltpu.VMEM((2, 8, tokens), F32),
            pltpu.VMEM((2, width, tokens), BF16),
            pltpu.VMEM((2, 2 * HEADS, tokens), F32),
            pltpu.VMEM((2, width, tokens), BF16),
            pltpu.VMEM((2, 2 * HEADS, tokens), F32),
            pltpu.VMEM((2, width, tokens), F32),
            pltpu.VMEM((width // 2, tokens), BF16),
            pltpu.VMEM((width // 2, tokens), BF16),
            pltpu.VMEM((HEADS, tokens), F32),
            pltpu.VMEM((HEADS, tokens), F32),
            pltpu.SMEM(block_table.shape, jnp.int32),
            pltpu.SMEM(shifts.shape, jnp.int32),
            pltpu.SemaphoreType.DMA((2 + len(operands),)),
            pltpu.SemaphoreType.DMA((17,)),
            pltpu.SemaphoreType.DMA((17,)),
        ],
        compiler_params=pltpu.CompilerParams(
            collective_id=0, has_side_effects=True, vmem_limit_bytes=56 * 1024 * 1024
        ),
        cost_estimate=pl.CostEstimate(
            flops=flops, bytes_accessed=12 * 1024 * 1024, transcendentals=2 * 1024 * 1024
        ),
    )(*small, *operands)
    return result.reshape(fine.shape)


def solution(mesh):
    placed = (
        P("tile", "narrow", None),
        P("tile", None, None),
        P("tile", None),
    ) + (P(),) * 12
    return jax.shard_map(
        functools.partial(local, mesh.shape["tile"], mesh.shape["narrow"]),
        mesh=mesh,
        in_specs=placed,
        out_specs=P("tile", "narrow", None),
        check_vma=False,
    )
```

```python
import functools

import jax
import jax.numpy as jnp
from jax import lax
from jax.experimental import pallas as pl
from jax.experimental.pallas import tpu as pltpu
from jax.sharding import PartitionSpec as P

WS = 8
HD = 64
HEADS = 8
PAIR = 2 * HD
CT = 128
NB = 8
HIDDEN = -1e30
UNSEEN = -1e29
MESH = pl.DeviceIdType.MESH
F32 = jnp.float32
BF16 = jnp.bfloat16


def dot(a, b):
    return jnp.dot(a, b, preferred_element_type=F32)


def rms_scale(values, gain_vec):
    mean_square = jnp.mean(values * values, axis=-1, keepdims=True)
    return values * lax.rsqrt(mean_square + 1e-06) * gain_vec


def one_hot_rows(index, count):
    lanes = lax.broadcasted_iota(jnp.int32, (index.shape[0], count), 1)
    return (lanes == index).astype(F32).astype(BF16)


def paired(q_t):
    zero = jnp.zeros((HD, q_t.shape[1]), q_t.dtype)
    upper = jnp.concatenate([q_t[:HD], zero], axis=1)
    lower = jnp.concatenate([zero, q_t[HD:]], axis=1)
    return jnp.concatenate([upper, lower], axis=0)


def unpaired(both, tokens):
    return jnp.concatenate([both[:HD, :tokens], both[HD:, tokens:]], axis=0)


def kernel(
    tiles,
    narrows,
    table_in,
    shifts_in,
    fine,
    coarse,
    attn_gain,
    w_query,
    w_key,
    w_value,
    w_out,
    coarse_key,
    coarse_value,
    mlp_gain,
    w_gate,
    w_up,
    w_down,
    out,
    ext,
    far,
    coarse_v,
    gain1_v,
    wq_v,
    wk_v,
    wv_v,
    wo_v,
    ck_v,
    cv_v,
    gain2_v,
    wg_v,
    wu_v,
    wd_v,
    keys_v,
    values_t,
    table_send,
    table_recv,
    o_send,
    st_send,
    o_recv,
    st_recv,
    own_o,
    far_send,
    far_recv,
    far_st_send,
    far_st_recv,
    table,
    shifts,
    load_sem,
    send_sem,
    recv_sem,
):
    s = lax.axis_index("tile")
    n = lax.axis_index("narrow")
    s_next, s_prev = lax.rem(s + 1, tiles), lax.rem(s + tiles - 1, tiles)
    s_next2, s_prev2 = lax.rem(s + 2, tiles), lax.rem(s + tiles - 2, tiles)
    n_next, n_prev = lax.rem(n + 1, narrows), lax.rem(n + narrows - 1, narrows)
    tokens, width = fine.shape
    half = WS * WS
    rows_dev = tokens // WS
    blocks = coarse.shape[0] // CT
    two_sides = narrows > 2

    barrier = pltpu.get_barrier_semaphore()
    for peer in (
        (s_next, n),
        (s_prev, n),
        (s_next2, n),
        (s_prev2, n),
        (s, n_next),
        (s, n_prev),
    ):
        pl.semaphore_signal(barrier, inc=1, device_id=peer, device_id_type=MESH)

    pairs = (
        (coarse, coarse_v),
        (coarse_key, ck_v),
        (coarse_value, cv_v),
        (table_in, table),
        (shifts_in, shifts),
        (fine, ext.at[pl.ds(0, tokens)]),
        (attn_gain, gain1_v),
        (w_query, wq_v),
        (w_key, wk_v),
        (w_value, wv_v),
        (w_out, wo_v),
        (mlp_gain, gain2_v),
        (w_gate, wg_v),
        (w_up, wu_v),
        (w_down, wd_v),
    )
    loads = [
        pltpu.make_async_copy(src, dst, load_sem.at[i]) for i, (src, dst) in enumerate(pairs)
    ]
    for i in (*range(3, 5), *range(3), *range(5, 8)):
        loads[i].start()

    def remote(slot, src, dst, peer):
        return pltpu.make_async_remote_copy(
            src_ref=src,
            dst_ref=dst,
            send_sem=send_sem.at[slot],
            recv_sem=recv_sem.at[slot],
            device_id=peer,
            device_id_type=MESH,
        )

    above, below, side, other = tokens, 2 * tokens, 3 * tokens, 5 * tokens
    pl.semaphore_wait(barrier, 6)
    even = lax.rem(s, 2) == 0
    peer_a = jnp.where(even, s_prev, s_next)
    peer_b = jnp.where(even, s_next, s_prev)
    at_a = pl.multiple_of(jnp.where(even, above, below), half)
    at_b = pl.multiple_of(jnp.where(even, below, above), half)
    to_a = remote(2, fine, ext.at[pl.ds(at_b, tokens)], (peer_a, n))
    to_b = remote(3, fine, ext.at[pl.ds(at_a, tokens)], (peer_b, n))
    to_far = remote(4, fine.at[pl.ds(0, half)], far, (s_prev2, n))
    sides = [remote(5, fine, ext.at[pl.ds(side, tokens)], (s, n_prev))]
    if two_sides:
        sides.append(remote(6, fine, ext.at[pl.ds(other, tokens)], (s, n_next)))
    for copy in (to_a, to_far, *sides):
        copy.start()
    for i in range(8, len(loads)):
        loads[i].start()

    loads[3].wait()
    loads[4].wait()
    total = blocks * tiles
    entries = []
    for i in range(NB):
        e = table[0, i] - (s - 1) * blocks
        e = jnp.where(e < 0, e + total, e)
        entries.append(jnp.where(e >= total, e - total, e))

    def block_bias(j):
        hit = entries[0] == j
        for e in entries[1:]:
            hit = hit | (e == j)
        return jnp.where(hit, 0.0, HIDDEN).astype(F32)

    bias = [block_bias(j) for j in range(3 * blocks)]
    row = lax.broadcasted_iota(jnp.int32, (16, tokens), 0)
    filled = jnp.zeros((16, tokens), F32)
    for b in range(blocks):
        filled = jnp.where(row == b, bias[2 * blocks + b], filled)
        filled = jnp.where(row == 8 + b, bias[b], filled)
    table_send[...] = filled

    table_copies = (
        remote(0, table_send.at[pl.ds(0, 8)], table_recv.at[0], (s_next, n)),
        remote(1, table_send.at[pl.ds(8, 8)], table_recv.at[1], (s_prev, n)),
    )
    for copy in table_copies:
        copy.start()
    shift_row = shifts[0]
    shift_col = shifts[1]

    for i in range(3):
        loads[i].wait()
    keys_v[...] = dot(coarse_v[...], ck_v[...]).astype(BF16)
    to_b.start()
    values_t[...] = dot(coarse_v[...], cv_v[...]).T.astype(BF16)

    for i in range(5, 10):
        loads[i].wait()

    def normed_of(raw):
        return rms_scale(raw.astype(F32), gain1_v[...]).astype(BF16)

    def queries_of(raw):
        queries = dot(normed_of(raw), wq_v[...]) * (1.0 / HD**0.5)
        return queries.T.astype(BF16)

    for copy in table_copies:
        copy.wait()
    early = (lax.broadcasted_iota(jnp.int32, (1, tokens), 1) >> 3) < shift_row

    def token_bias(upper, lower):
        rows = []
        for x, y in zip(upper, lower):
            one = jnp.where(early, x, y)
            rows.append(jnp.concatenate([one, one], axis=1))
        return rows

    by_prev = [table_recv[0, pl.ds(b, 1), :] for b in range(blocks)]
    by_own = bias[blocks : 2 * blocks]
    by_next = [table_recv[1, pl.ds(b, 1), :] for b in range(blocks)]
    by_none = [HIDDEN] * blocks

    def attend(pair, q_pair, biases):
        at = slice(pair * PAIR, (pair + 1) * PAIR)
        scores = dot(keys_v[:, at], q_pair)
        parts = [scores[b * CT : (b + 1) * CT] for b in range(blocks)]
        top = None
        for part, hide in zip(parts, biases):
            high = jnp.max(part, axis=0, keepdims=True) + hide
            top = high if top is None else jnp.maximum(top, high)
        unseen = top < UNSEEN
        parts = [
            jnp.exp(part - jnp.where(unseen, -HIDDEN, top - hide))
            for part, hide in zip(parts, biases)
        ]
        amount = sum(jnp.sum(part, axis=0, keepdims=True) for part in parts)
        mixed = dot(values_t[at, :], jnp.concatenate(parts, axis=0).astype(BF16))
        return top, amount, mixed

    def split_heads(rows):
        halves = []
        for row in rows:
            halves += [row[:, :tokens], row[:, tokens:]]
        return jnp.concatenate(halves, axis=0)

    def cross(q_t, biases, store):
        tops, amounts = [], []
        for pair in range(HEADS // 2):
            q_pair = paired(q_t[pair * PAIR : (pair + 1) * PAIR])
            top, amount, mixed = attend(pair, q_pair, biases)
            store(pair, unpaired(mixed, tokens))
            tops.append(top)
            amounts.append(amount)
        return split_heads(tops), split_heads(amounts)

    def neighbour(slot, raw, biases, peer):
        def store(pair, mixed):
            o_send[slot, pl.ds(pair * PAIR, PAIR), :] = mixed.astype(BF16)

        top, amount = cross(queries_of(raw), biases, store)
        st_send[slot, pl.ds(0, HEADS), :] = top
        st_send[slot, pl.ds(HEADS, HEADS), :] = amount
        copies = [
            remote(7 + 2 * slot, st_send.at[slot], st_recv.at[slot], peer),
            remote(8 + 2 * slot, o_send.at[slot], o_recv.at[slot], peer),
        ]
        for copy in copies:
            copy.start()
        return copies

    def keep(pair, mixed):
        own_o[0, pl.ds(pair * PAIR, PAIR), :] = mixed

    forwards = []

    def forward(slot, at, place):
        src = ext.at[pl.ds(pl.multiple_of(at, half), half)]
        dst = ext.at[pl.ds(pl.multiple_of(side + place, half), half)]
        copies = [remote(slot, src, dst, (s, n_prev))]
        if two_sides:
            dst = ext.at[pl.ds(pl.multiple_of(other + place, half), half)]
            copies.append(remote(slot + 1, src, dst, (s, n_next)))
        for copy in copies:
            copy.start()
        return copies

    def choose(x, y):
        return [jnp.where(even, a, b) for a, b in zip(x, y)]

    last_above, first_below = above + tokens - half, below
    to_a.wait_recv()
    forwards += forward(
        13,
        jnp.where(even, last_above, first_below),
        jnp.where(even, tokens, tokens + half),
    )
    part_copies = neighbour(
        0,
        ext[pl.ds(at_a, tokens), :],
        token_bias(choose(by_none, by_own), choose(by_prev, by_next)),
        (peer_a, n),
    )
    to_b.wait_recv()
    forwards += forward(
        15,
        jnp.where(even, first_below, last_above),
        jnp.where(even, tokens + half, tokens),
    )
    part_copies += neighbour(
        1,
        ext[pl.ds(at_b, tokens), :],
        token_bias(choose(by_own, by_none), choose(by_next, by_prev)),
        (peer_b, n),
    )
    lane = lax.broadcasted_iota(jnp.int32, (1, tokens), 1)
    left_half = lane < half
    far_early = ((lane & (half - 1)) >> 3) < shift_row
    far_bias = [jnp.where(far_early, x, HIDDEN) for x in by_next]
    quadrant = (lax.broadcasted_iota(jnp.int32, (PAIR, tokens), 0) < HD) == (
        lax.broadcasted_iota(jnp.int32, (PAIR, tokens), 1) < half
    )
    quadrant = jnp.where(quadrant, 1.0, 0.0).astype(BF16)
    to_far.wait_recv()
    far_raw = far[...]
    far_q = queries_of(jnp.concatenate([far_raw, far_raw], axis=0))
    tops, amounts = [], []
    for pair in range(HEADS // 2):
        at = slice(pair * PAIR, (pair + 1) * PAIR)
        top, amount, mixed = attend(pair, far_q[at] * quadrant, far_bias)
        far_send[pl.ds(pair * HD, HD), :] = jnp.where(left_half, mixed[:HD], mixed[HD:]).astype(
            BF16
        )
        tops.append(top)
        amounts.append(amount)
    far_st_send[...] = jnp.concatenate(tops + amounts, axis=0)
    far_copies = [
        remote(11, far_st_send, far_st_recv, (s_next2, n)),
        remote(12, far_send, far_recv, (s_next2, n)),
    ]
    for copy in far_copies:
        copy.start()
    part_copies += far_copies

    own_q = queries_of(ext[pl.ds(0, tokens), :])
    own_top, own_amount = cross(own_q, token_bias(by_prev, by_own), keep)

    for copy in sides:
        copy.wait_recv()
    for copy in forwards:
        copy.wait_recv()
    near = 6 * half
    k = lax.broadcasted_iota(jnp.int32, (near, 1), 0)
    row = (k >> 4) + shift_row - WS
    col = (k & 15) + shift_col - WS
    is_above, is_below = row < 0, row >= rows_dev
    is_left, is_right = col < 0, col >= WS
    row_in = jnp.where(is_above, row + rows_dev, jnp.where(is_below, row - rows_dev, row))
    col_in = jnp.where(is_left, col + WS, jnp.where(is_right, col - WS, col))
    middle = jnp.where(is_above, above, jnp.where(is_below, below, 0))
    beside = jnp.where(
        is_above, tokens - half, jnp.where(is_below, tokens + half, 0)
    ) + jnp.where(is_left, other if two_sides else side, side)
    place = jnp.where(is_left | is_right, beside, middle) + row_in * WS + col_in
    around = dot(one_hot_rows(place, ext.shape[0]), ext[...])
    normed = normed_of(around)
    keys_fine = dot(normed, wk_v[...]).astype(BF16)
    values_fine_t = dot(normed, wv_v[...]).T.astype(BF16)

    def label(row, col):
        g = s * rows_dev + row
        g = jnp.where(g < 0, g + rows_dev * tiles, g)
        g = jnp.where(g >= rows_dev * tiles, g - rows_dev * tiles, g)
        h = n * WS + col
        h = jnp.where(h < 0, h + WS * narrows, h)
        h = jnp.where(h >= WS * narrows, h - WS * narrows, h)
        window = ((row - shift_row + WS) >> 3) * 2 + ((col - shift_col + WS) >> 3)
        return window * 4 + jnp.where(g < shift_row, 2, 0) + jnp.where(h < shift_col, 1, 0)

    k = lax.broadcasted_iota(jnp.int32, (near, tokens), 0)
    t = lax.broadcasted_iota(jnp.int32, (near, tokens), 1)
    same = label((k >> 4) + shift_row - WS, (k & 15) + shift_col - WS) == label(t >> 3, t & 7)
    hide = jnp.where(same, 0.0, HIDDEN).astype(F32)
    hide = jnp.concatenate([hide, hide], axis=1)
    tops, amounts = [], []
    for pair in range(HEADS // 2):
        at = slice(pair * PAIR, (pair + 1) * PAIR)
        scores = dot(keys_fine[:, at], paired(own_q[at])) + hide
        top = jnp.max(scores, axis=0, keepdims=True)
        weights = jnp.exp(scores - top)
        tops.append(top)
        amounts.append(jnp.sum(weights, axis=0, keepdims=True))
        mixed = dot(values_fine_t[at, :], weights.astype(BF16))
        own_o[1, pl.ds(pair * PAIR, PAIR), :] = unpaired(mixed, tokens)
    self_top, self_amount = split_heads(tops), split_heads(amounts)

    for i in range(10, len(loads)):
        loads[i].wait()
    for copy in part_copies:
        copy.wait()
    for copy in (to_a, to_b, to_far, *sides, *forwards):
        copy.wait_send()

    def swapped(x):
        return jnp.concatenate([x[:, half:], x[:, :half]], axis=1)

    def far_rows(first, absent):
        straight = far_st_recv[pl.ds(first, HEADS // 2), :]
        crossed = swapped(straight)
        rows = []
        for i in range(HEADS // 2):
            rows += [straight[i : i + 1], crossed[i : i + 1]]
        return jnp.where(left_half, jnp.concatenate(rows, axis=0), absent)

    all_tops = [own_top, self_top] + [st_recv[i, pl.ds(0, HEADS), :] for i in range(2)]
    all_tops.append(far_rows(0, HIDDEN))
    all_amounts = [own_amount, self_amount] + [
        st_recv[i, pl.ds(HEADS, HEADS), :] for i in range(2)
    ]
    all_amounts.append(far_rows(HEADS // 2, 0.0))
    top = functools.reduce(jnp.maximum, all_tops)
    scales = [jnp.exp(x - top) for x in all_tops]
    amount = sum(a * b for a, b in zip(scales, all_amounts))
    scales = [x / amount for x in scales]
    heads = []
    for h in range(HEADS):
        at = pl.ds(h * HD, HD)
        mixed = own_o[0, at, :] * scales[0][h : h + 1] + own_o[1, at, :] * scales[1][h : h + 1]
        distant = far_recv[pl.ds(h // 2 * HD, HD), :].astype(F32)
        if h % 2:
            distant = swapped(distant)
        mixed = mixed + distant * scales[4][h : h + 1]
        for i in range(2):
            mixed = mixed + o_recv[i, at, :].astype(F32) * scales[2 + i][h : h + 1]
        heads.append(mixed)
    head_out = jnp.concatenate(heads, axis=0).T.astype(BF16)
    mid = ext[pl.ds(0, tokens), :].astype(F32) + dot(head_out, wo_v[...])
    normed_mid = rms_scale(mid, gain2_v[...]).astype(BF16)
    gate = dot(normed_mid, wg_v[...])
    up = dot(normed_mid, wu_v[...])
    hidden = (gate * lax.logistic(gate) * up).astype(BF16)
    out[...] = (mid + dot(hidden, wd_v[...])).astype(BF16)


def local(
    tiles,
    narrows,
    fine,
    coarse,
    block_table,
    shifts,
    attn_gain,
    w_query,
    w_key,
    w_value,
    w_out,
    coarse_key,
    coarse_value,
    mlp_gain,
    w_gate,
    w_up,
    w_down,
):
    width = fine.shape[-1]
    tokens = fine.shape[0] * fine.shape[1]
    flat = fine.reshape(tokens, width)
    coarse_flat = coarse.reshape(-1, coarse.shape[-1])
    keys = coarse_flat.shape[0]
    gain1 = attn_gain.reshape(1, width)
    gain2 = mlp_gain.reshape(1, width)
    anywhere = pl.BlockSpec(memory_space=pltpu.HBM)

    def room(like):
        return pltpu.VMEM(like.shape, like.dtype)

    small = tuple(
        pltpu.with_memory_space_constraint(x, pltpu.HBM) for x in (block_table, shifts)
    )
    operands = tuple(pltpu.with_memory_space_constraint(x, pltpu.HBM) for x in (
        flat,
        coarse_flat,
        gain1,
        w_query,
        w_key,
        w_value,
        w_out,
        coarse_key,
        coarse_value,
        gain2,
        w_gate,
        w_up,
        w_down,
    ))
    flops = 2 * keys * coarse.shape[-1] * 2 * width + 6 * tokens * width * w_gate.shape[-1]
    result = pl.pallas_call(
        functools.partial(kernel, tiles, narrows),
        out_shape=pltpu.VMEM((tokens, width), fine.dtype),
        in_specs=[anywhere] * (2 + len(operands)),
        out_specs=pl.BlockSpec(memory_space=pltpu.VMEM),
        scratch_shapes=[
            pltpu.VMEM(((7 if narrows > 2 else 5) * tokens, width), BF16),
            pltpu.VMEM((WS * WS, width), BF16),
        ]
        + [room(x) for x in operands[1:]]
        + [
            pltpu.VMEM((keys, width), BF16),
            pltpu.VMEM((width, keys), BF16),
            pltpu.VMEM((16, tokens), F32),
            pltpu.VMEM((2, 8, tokens), F32),
            pltpu.VMEM((2, width, tokens), BF16),
            pltpu.VMEM((2, 2 * HEADS, tokens), F32),
            pltpu.VMEM((2, width, tokens), BF16),
            pltpu.VMEM((2, 2 * HEADS, tokens), F32),
            pltpu.VMEM((2, width, tokens), F32),
            pltpu.VMEM((width // 2, tokens), BF16),
            pltpu.VMEM((width // 2, tokens), BF16),
            pltpu.VMEM((HEADS, tokens), F32),
            pltpu.VMEM((HEADS, tokens), F32),
            pltpu.SMEM(block_table.shape, jnp.int32),
            pltpu.SMEM(shifts.shape, jnp.int32),
            pltpu.SemaphoreType.DMA((2 + len(operands),)),
            pltpu.SemaphoreType.DMA((17,)),
            pltpu.SemaphoreType.DMA((17,)),
        ],
        compiler_params=pltpu.CompilerParams(
            collective_id=0, has_side_effects=True, vmem_limit_bytes=56 * 1024 * 1024
        ),
        cost_estimate=pl.CostEstimate(
            flops=flops, bytes_accessed=12 * 1024 * 1024, transcendentals=2 * 1024 * 1024
        ),
    )(*small, *operands)
    return result.reshape(fine.shape)


def solution(mesh):
    placed = (
        P("tile", "narrow", None),
        P("tile", None, None),
        P("tile", None),
    ) + (P(),) * 12
    return jax.shard_map(
        functools.partial(local, mesh.shape["tile"], mesh.shape["narrow"]),
        mesh=mesh,
        in_specs=placed,
        out_specs=P("tile", "narrow", None),
        check_vma=False,
    )
```
